256 devices in a mesh: unit: 64 (over y, z, core), vec: 4 (over x).
Axes of the slice: x: 4, y: 4, z: 8, core: 2. Of those that a mesh axis runs over, the one named last changes fastest.
Arguments:
- tangents: bfloat16 [262144, 512], P('unit', 'vec'), may hold values from -120 to 120, as said below
- state: float32 [262144], P('unit'), may hold values from -6 to 6
- gain: float32 [262144], P('unit'), may hold values from 0.8 to 3
- local_w: bfloat16 [16384, 128, 128], P('unit'), may hold values from -0.15625 to 0.15625
- local_row: int32 [16384], P('unit'), may hold values from 0 to 31
- local_col: int32 [16384], P('unit'), may hold values from 0 to 31
- remote_w: bfloat16 [4096, 128, 128], P('unit'), may hold values from -0.15625 to 0.15625
- remote_row: int32 [4096], P('unit'), may hold values from 0 to 31
- remote_owner: int32 [4096, 1], P('unit'), may hold values from 0 to 63; in each aligned block of 64 rows (0 to 63, 64 to 127, ...) at most 2 rows name the same one
- remote_offset: int32 [4096], P('unit'), may hold values from 0 to 31
Outputs:
- new_tangents: bfloat16 [262144, 512], P('unit', 'vec')
- exponents: float32 [512], replicated
The draws below stay inside these ranges and needn't reach their ends.
Inputs may be any that keep to these rules, and one draw needn't show every extreme that they name: `tangents`: the 512 columns are linearly independent. `remote_owner`: among the 64 second-part blocks of one shard no owner is named more than 2 times, a bound that some block reaches.
All inputs are finite; a program needn't handle non-finite values.
Results may differ from the reference program's by a relative error of at most 0.003.
The reference program's roundings to bfloat16 on the way (of `scaled`, `stepped` and `inverse_up`) count: a program that leaves them out, or rounds other values in their place, can miss the bound.
Values may be sent and summed in bfloat16 or wider, within the bound.
No kernel may reach another device: no remote copies, remote signals or barrier semaphores. Data moves between devices by JAX's collectives and lax.ppermute only.
A program may use at most 128 MiB of HBM per device.

```python
import math
import jax
import jax.numpy as jnp
import numpy as np
from jax import lax

BLK = 128
K = 512
BR_DEV = 32
LOC_DEV = 256
REM_DEV = 64
CAP = 2
N = 262144
N_UNIT = 64


def draw_tangents(key, part):
    key = jax.random.fold_in(key, 11)
    base_key, row_key, col_key = jax.random.split(key, 3)
    unit_total = BR_DEV * BLK * N_UNIT
    positions = jnp.arange(unit_total, dtype=jnp.float32) / unit_total
    row_scale = jnp.exp(math.log(3.0) * positions + jax.random.uniform(row_key, (unit_total,), jnp.float32, 0.0, math.log(10.0)))
    col_scale = jnp.exp(jax.random.uniform(col_key, (K,), jnp.float32, 0.0, math.log(10.0)))
    entries = jax.random.truncated_normal(base_key, -4.0, 4.0, (unit_total, K), jnp.float32)
    return (0.1 * entries * row_scale[:, None] * col_scale[None, :]).astype(jnp.bfloat16)


def touch_ends(values, own_key, least, high):
    longest = values.shape.index(max(values.shape))
    spots = []
    for shift in (0, 1):
        where = [jax.random.randint(jax.random.fold_in(own_key, axis), (), 0, length) for axis, length in enumerate(values.shape)]
        where[longest] = (where[longest] + shift) % values.shape[longest]
        spots.append(tuple(where))
    return values.at[spots[0]].set(least).at[spots[1]].set(high)


def block_levels(rng, extent, cuts, low, high):
    factor_of, own = 1.0, jax.random.fold_in(rng, 6)
    for axis_at, parts in cuts:
        draws = jnp.exp(jax.random.uniform(jax.random.fold_in(own, axis_at), (parts,), jnp.float32, low / len(cuts), high / len(cuts)))
        factor_of = factor_of * jnp.repeat(draws, extent[axis_at] // parts).reshape([-1 if axis == axis_at else 1 for axis in range(len(extent))])
    return factor_of


def shared_out(stream_key, own, number, rows, amount, top, limit, slope):
    ranking = jax.random.permutation(stream_key, amount)
    crowded, usual = portions_of(amount, rows * top, limit, slope, True), portions_of(amount, rows * top, limit, slope, False)
    places = jnp.arange(amount)

    def named(lengths, offset_by):
        used = int((lengths > 0).sum())
        fixed = max(1, used // 4)
        shifted = fixed + (places - fixed + offset_by * (used - fixed)) % max(1, amount - fixed)
        return jnp.zeros((amount,), jnp.int32).at[ranking[jnp.where(places < fixed, places, shifted)]].set(jnp.asarray(lengths, jnp.int32))

    lengths = jnp.where(number % 4 == 0, named(crowded, number // 4), named(usual, number - number // 4 - 1))
    mixed = jax.random.permutation(jax.random.fold_in(own, 3), amount)
    source_of, taker = mixed[0:amount // 2 * 2:2], mixed[1:amount // 2 * 2:2]
    margin = jnp.minimum(lengths[source_of] - 1, limit - lengths[taker]) // 2
    margin = jnp.where((source_of == ranking[0]) | (taker == ranking[0]) | (lengths[taker] == 0), 0, jnp.maximum(margin, 0))
    shifted = jax.random.randint(jax.random.fold_in(own, 4), (amount // 2,), 0, 1 << 20) % (margin + 1)
    lengths = lengths.at[source_of].add(-shifted).at[taker].add(shifted)
    members = jnp.searchsorted(jnp.cumsum(lengths), jnp.arange(rows * top), side="right").astype(jnp.int32)
    listing = members.reshape(top, rows).T
    listing = listing[jax.random.permutation(jax.random.fold_in(own, 1), rows)]
    offset_by = jax.random.randint(jax.random.fold_in(own, 2), (rows, 1), 0, top)
    return jnp.take_along_axis(listing, (jnp.arange(top)[None, :] + offset_by) % top, axis=1)


def portions_of(count, total, limit, lean, full):
    weights = [(1 << 20) // math.isqrt(rank ** lean) + 1 for rank in range(1, count + 1)]
    largest = limit if full else min(limit, max(-(-total // count), total * weights[0] // sum(weights)))
    least = 1 if total - largest >= count - 1 else 0
    given, spare = [largest] + [least] * (count - 1), total - largest - least * (count - 1)
    while spare > 0:
        movable = [i for i in range(1, count) if given[i] < largest] or [i for i in range(1, count) if given[i] < limit]
        mass, budget = sum([weights[i] for i in movable]), spare
        for i in movable:
            more = min(limit - given[i], max(1, budget * weights[i] // mass), spare)
            given[i] = given[i] + more
            spare = spare - more
    return np.array(given)


def gaussian(own_key, dims, width, most, cuts=(), kind=jnp.bfloat16):
    values = jax.random.normal(own_key, dims, jnp.float32) * width
    if len(cuts) > 0:
        values = block_levels(own_key, dims, cuts, -0.22, 0.18) * values
    return jnp.clip(values, min=-most, max=most).astype(kind)


def setup_inputs(seed: int = 0) -> dict:
    keys = jax.random.split(jax.random.key(seed), 11)
    tangents = draw_tangents(jax.random.fold_in(keys[10], 71), 0)
    state = gaussian(keys[1], (N,), 1.0, 6.0, ((0, 64),), jnp.float32)
    gain = jnp.clip(jnp.exp(math.log(3.0) - 1.3217558 * jax.random.uniform(keys[2], (N,), jnp.float32) ** block_levels(keys[2], (N,), ((0, 64),), -0.2, 0.2)), 0.8, 3.0)
    local_w = gaussian(keys[3], (LOC_DEV * N_UNIT, BLK, BLK), (10 * BLK) ** -0.5, 0.15625, ((0, 64),))
    local_row = touch_ends(jax.random.randint(keys[4], (LOC_DEV * N_UNIT,), 0, BR_DEV), jax.random.fold_in(keys[4], 1), 0, BR_DEV - 1).astype(jnp.int32)
    local_col = touch_ends(jax.random.randint(keys[5], (LOC_DEV * N_UNIT,), 0, BR_DEV), jax.random.fold_in(keys[5], 1), 0, BR_DEV - 1).astype(jnp.int32)
    remote_w = gaussian(keys[6], (REM_DEV * N_UNIT, BLK, BLK), (10 * BLK) ** -0.5, 0.15625, ((0, 64),))
    remote_row = touch_ends(jax.random.randint(keys[7], (REM_DEV * N_UNIT,), 0, BR_DEV), jax.random.fold_in(keys[7], 1), 0, BR_DEV - 1).astype(jnp.int32)
    remote_owner_keys = jax.random.split(jax.random.fold_in(keys[8], 1), (REM_DEV * N_UNIT) // REM_DEV)
    remote_owner_turns = jax.random.permutation(jax.random.fold_in(keys[8], 3), (REM_DEV * N_UNIT) // REM_DEV)
    remote_owner = jax.vmap(lambda own, number: shared_out(jax.random.fold_in(keys[8], 2), own, number, REM_DEV, N_UNIT, 1, CAP, 2))(remote_owner_keys, remote_owner_turns).reshape((REM_DEV * N_UNIT, 1))
    remote_offset = touch_ends(jax.random.randint(keys[9], (REM_DEV * N_UNIT,), 0, BR_DEV), jax.random.fold_in(keys[9], 1), 0, BR_DEV - 1).astype(jnp.int32)
    return dict(tangents=tangents, state=state, gain=gain, local_w=local_w, local_row=local_row, local_col=local_col, remote_w=remote_w, remote_row=remote_row, remote_owner=remote_owner, remote_offset=remote_offset)


time_step = 0.5

def reference(tangents, state, gain, local_w, local_row, local_col, remote_w, remote_row, remote_owner, remote_offset):
    slopes = gain * (1.0 - jnp.tanh(gain * state) ** 2)
    scaled = (slopes[:, None] * tangents.astype(jnp.float32)).astype(jnp.bfloat16)
    pieces = scaled.reshape(BR_DEV * N_UNIT, BLK, K)
    owner_list = remote_owner[:, 0]

    def one_shard(shard_id):
        first_row = shard_id * BR_DEV
        own_local = lax.dynamic_slice_in_dim(local_w, shard_id * LOC_DEV, LOC_DEV, 0)
        rows_local = lax.dynamic_slice_in_dim(local_row, shard_id * LOC_DEV, LOC_DEV, 0)
        cols_local = lax.dynamic_slice_in_dim(local_col, shard_id * LOC_DEV, LOC_DEV, 0)
        near_blocks = pieces[(first_row + cols_local).astype(jnp.int32)]
        local_terms = jnp.einsum('bij,bjk->bik', own_local.astype(jnp.float32), near_blocks.astype(jnp.float32))
        local_sum = jax.ops.segment_sum(local_terms, rows_local, num_segments=BR_DEV)
        own_remote = lax.dynamic_slice_in_dim(remote_w, shard_id * REM_DEV, REM_DEV, 0)
        rows_remote = lax.dynamic_slice_in_dim(remote_row, shard_id * REM_DEV, REM_DEV, 0)
        owners = lax.dynamic_slice_in_dim(owner_list, shard_id * REM_DEV, REM_DEV, 0)
        offsets = lax.dynamic_slice_in_dim(remote_offset, shard_id * REM_DEV, REM_DEV, 0)
        far_blocks = pieces[(owners * BR_DEV + offsets).astype(jnp.int32)]
        far_terms = jnp.einsum('bij,bjk->bik', own_remote.astype(jnp.float32), far_blocks.astype(jnp.float32))
        far_sum = jax.ops.segment_sum(far_terms, rows_remote, num_segments=BR_DEV)
        coupled = (local_sum + far_sum).reshape(BR_DEV * BLK, K)
        own_tangents = lax.dynamic_slice_in_dim(tangents, first_row * BLK, BR_DEV * BLK, 0)
        stepped = (1.0 - time_step) * own_tangents.astype(jnp.float32) + time_step * coupled
        return stepped.astype(jnp.bfloat16)
    shard_ids = jnp.arange(N_UNIT, dtype=jnp.int32)
    stepped_all = lax.map(one_shard, shard_ids)
    flat_rows = stepped_all.reshape(N, K)
    gram_matrix = jnp.dot(flat_rows.T.astype(jnp.float32), flat_rows.astype(jnp.float32), preferred_element_type=jnp.float32) / N
    lower_factor = jnp.linalg.cholesky(gram_matrix)
    identity_m = jnp.eye(K, dtype=jnp.float32)
    inverse_low = jax.scipy.linalg.solve_triangular(lower_factor, identity_m, lower=True)
    inverse_up = inverse_low.T.astype(jnp.bfloat16)

    def renew(block_rows):
        return jnp.dot(block_rows.astype(jnp.float32), inverse_up.astype(jnp.float32), preferred_element_type=jnp.float32).astype(jnp.bfloat16)
    new_tangents = lax.map(renew, stepped_all).reshape(N, K)
    exponents = jnp.log(jnp.diagonal(lower_factor))
    return (new_tangents, exponents)
```

```python
import functools

import jax
import jax.numpy as jnp
from jax import lax
from jax.experimental import pallas as pl
from jax.experimental.pallas import tpu as pltpu
from jax.sharding import PartitionSpec as P

time_step = 0.5
HIGHEST = lax.Precision.HIGHEST
MIB = 1024 * 1024


def split_dot(left, right, left_dim, right_dim):
    return lax.dot_general(
        left,
        right,
        (((left_dim,), (right_dim,)), ((), ())),
        precision=HIGHEST,
        preferred_element_type=jnp.float32,
    )


def local_kernel(row_ref, col_ref, w_ref, x_ref, t_ref, acc_ref):
    step = pl.program_id(0)
    count = w_ref.shape[0]

    @pl.when(step == 0)
    def _():
        acc_ref[...] = t_ref[...].astype(jnp.float32)

    @pl.loop(0, count // 8)
    def _(group):
        for inner in range(8):
            block = group * 8 + inner
            row = row_ref[step * count + block]
            col = col_ref[step * count + block]
            acc_ref[row] += jnp.dot(w_ref[block], x_ref[col], preferred_element_type=jnp.float32)


def local_product(local_row, local_col, local_w, pieces, tangents):
    count, side, _ = local_w.shape
    block_rows, _, width = pieces.shape
    chunk = 32
    whole = lambda i, *_: (0, 0, 0)
    return pl.pallas_call(
        local_kernel,
        grid_spec=pltpu.PrefetchScalarGridSpec(
            num_scalar_prefetch=2,
            grid=(count // chunk,),
            in_specs=[
                pl.BlockSpec((chunk, side, side), lambda i, *_: (i, 0, 0)),
                pl.BlockSpec((block_rows, side, width), whole),
                pl.BlockSpec((block_rows, side, width), whole),
            ],
            out_specs=pl.BlockSpec((block_rows, side, width), whole),
        ),
        out_shape=jax.ShapeDtypeStruct((block_rows, side, width), jnp.float32),
        compiler_params=pltpu.CompilerParams(vmem_limit_bytes=16 * MIB),
        cost_estimate=pl.CostEstimate(
            flops=2 * count * side * side * width, bytes_accessed=14 * MIB, transcendentals=0
        ),
        name="local_blocks",
    )(local_row, local_col, local_w, pieces, tangents)


def column_of(row, side):
    return jnp.broadcast_to(row, (side, side)).T


def spread_kernel(state_ref, gain_ref, t_ref, ask_ref, pieces_ref, spread_ref):
    block_rows, side, width = t_ref.shape
    half = side // 2
    gain = gain_ref[...]
    slopes = gain * (1.0 - jnp.tanh(gain * state_ref[...]) ** 2)
    for p in range(block_rows):
        slope = column_of(slopes[p : p + 1, :], side)
        pieces_ref[p] = (slope * t_ref[p].astype(jnp.float32)).astype(jnp.bfloat16)
    for h in range(2):
        for g in range(block_rows // 16):
            group = pieces_ref[16 * g : 16 * g + 16, h * half : (h + 1) * half, :]
            at = h * block_rows + 16 * g
            spread_ref[:, at : at + 16, :] = jnp.swapaxes(group, 0, 1)
    units, rows, _ = spread_ref.shape
    extra = rows - 2 * block_rows
    spread_ref[:, 2 * block_rows :, :] = jnp.broadcast_to(
        ask_ref[...].reshape(1, 1, width), (units, extra, width)
    )


def spread_pieces(state, gain, blocks, ask, units):
    block_rows, side, width = blocks.shape
    rows = 2 * block_rows + 8
    vmem = pl.BlockSpec(memory_space=pltpu.VMEM)
    return pl.pallas_call(
        spread_kernel,
        in_specs=[vmem] * 4,
        out_specs=[vmem] * 2,
        out_shape=[
            jax.ShapeDtypeStruct((block_rows, side, width), jnp.bfloat16),
            jax.ShapeDtypeStruct((units, rows, width), jnp.bfloat16),
        ],
        compiler_params=pltpu.CompilerParams(vmem_limit_bytes=16 * MIB),
        cost_estimate=pl.CostEstimate(
            flops=4 * MIB, bytes_accessed=4 * MIB, transcendentals=block_rows * side
        ),
        name="spread_pieces",
    )(state.reshape(block_rows, side), gain.reshape(block_rows, side), blocks, ask)


def pick_kernel(block_rows, index_ref, table_ref, out_ref):
    shards, rows, width = out_ref.shape
    owners = table_ref.shape[0]
    depth = owners * block_rows
    table = jnp.concatenate(
        [
            table_ref[:, h * block_rows : (h + 1) * block_rows, :].reshape(depth, width)
            for h in range(2)
        ],
        axis=1,
    )
    index = jnp.concatenate(
        [column_of(index_ref[0, g : g + 1, :], width) for g in range(index_ref.shape[1])], axis=0
    ).astype(jnp.int32)
    lane = lax.broadcasted_iota(jnp.int32, index.shape, 1)
    hot = jnp.concatenate(
        [(index == lane + width * k).astype(jnp.bfloat16) for k in range(depth // width)], axis=1
    )
    found = jnp.dot(hot, table, preferred_element_type=jnp.float32).astype(jnp.bfloat16)
    found = found.reshape(shards, rows // 2, 2 * width)
    out_ref[:, : rows // 2, :] = found[:, :, :width]
    out_ref[:, rows // 2 :, :] = found[:, :, width:]


def pick_rows(index, table, block_rows):
    units, far_count = index.shape
    width = table.shape[-1]
    steps = 4
    lines = units * far_count // width // steps
    return pl.pallas_call(
        functools.partial(pick_kernel, block_rows),
        grid=(steps,),
        in_specs=[
            pl.BlockSpec((1, lines, width), lambda i: (i, 0, 0)),
            pl.BlockSpec(table.shape, lambda i: (0, 0, 0)),
        ],
        out_specs=pl.BlockSpec((units // steps, 2 * far_count, width), lambda i: (i, 0, 0)),
        out_shape=jax.ShapeDtypeStruct((units, 2 * far_count, width), jnp.bfloat16),
        compiler_params=pltpu.CompilerParams(vmem_limit_bytes=32 * MIB),
        cost_estimate=pl.CostEstimate(
            flops=4_000_000_000, bytes_accessed=4 * MIB, transcendentals=0
        ),
        name="pick_rows",
    )(index.reshape(steps, lines, width), table)


def far_kernel(own_ref, row_ref, w_ref, acc_in_ref, arrived_ref, out_ref, *rest):
    part_refs, (acc_ref, x_ref) = rest[:-2], rest[-2:]
    count = w_ref.shape[0]
    units = arrived_ref.shape[0]
    acc_ref[...] = acc_in_ref[...]
    for g in range(count // 16):
        for h in range(2):
            at = h * count + 16 * g
            x_ref[16 * g : 16 * g + 16, h * units : (h + 1) * units, :] = jnp.swapaxes(
                arrived_ref[:, at : at + 16, :], 0, 1
            )
        for inner in range(16):
            block = 16 * g + inner
            row = row_ref[block]
            acc_ref[row] += jnp.dot(w_ref[block], x_ref[block], preferred_element_type=jnp.float32)
    out_ref[...] = (time_step * acc_ref[...]).astype(jnp.bfloat16)
    parts = len(part_refs)
    for k in range(parts):
        share = part_refs[k].shape[0]
        part_refs[k][...] = out_ref[pl.ds(lax.rem(own_ref[0] + k, parts) * share, share)]


def far_product(own, remote_row, remote_w, acc, arrived, parts):
    count, side, _ = remote_w.shape
    block_rows, _, width = acc.shape
    vmem = pl.BlockSpec(memory_space=pltpu.VMEM)
    return pl.pallas_call(
        far_kernel,
        in_specs=[pl.BlockSpec(memory_space=pltpu.SMEM)] * 2 + [vmem] * 3,
        out_specs=[vmem] * (1 + parts),
        out_shape=[jax.ShapeDtypeStruct((block_rows, side, width), jnp.bfloat16)]
        + [jax.ShapeDtypeStruct((block_rows // parts, side, width), jnp.bfloat16)] * parts,
        scratch_shapes=[
            pltpu.VMEM((block_rows, side, width), jnp.float32),
            pltpu.VMEM((count, side, width), jnp.bfloat16),
        ],
        compiler_params=pltpu.CompilerParams(vmem_limit_bytes=20 * MIB),
        cost_estimate=pl.CostEstimate(
            flops=2 * count * side * side * width, bytes_accessed=8 * MIB, transcendentals=0
        ),
        name="far_blocks",
    )(own, remote_row, remote_w, acc, arrived)


def cross(left, right):
    return lax.dot_general(
        left, right, (((0,), (0,)), ((), ())), preferred_element_type=jnp.float32
    )


def gram_kernel(own_ref, *refs):
    parts = len(refs) // 2
    x_refs, out_refs = refs[:parts], refs[parts:]
    side = x_refs[0].shape[1]
    half = side // 2
    for k in range(parts):
        device = lax.rem(own_ref[0] + k, parts)
        here, after, across = (x_refs[(-k - step) % parts][...] for step in (0, 1, 2))
        products = cross(here, jnp.concatenate([here, after, across], axis=1))
        out_refs[k][:side, :] = products[:, :side]
        out_refs[k][side : 2 * side, :] = products[:, side : 2 * side]
        last = products[:, 2 * side :]
        out_refs[k][2 * side :, :] = jnp.where(device < 2, last[:half], last.T[half:])


def gram_quarters(own, row_parts):
    parts = len(row_parts)
    rows, side = row_parts[0].shape
    vmem = pl.BlockSpec(memory_space=pltpu.VMEM)
    return pl.pallas_call(
        gram_kernel,
        in_specs=[pl.BlockSpec(memory_space=pltpu.SMEM)] + [vmem] * parts,
        out_specs=[vmem] * parts,
        out_shape=[jax.ShapeDtypeStruct((2 * side + side // 2, side), jnp.float32)] * parts,
        compiler_params=pltpu.CompilerParams(vmem_limit_bytes=16 * MIB),
        cost_estimate=pl.CostEstimate(
            flops=6 * parts * rows * side * side, bytes_accessed=2 * MIB, transcendentals=0
        ),
        name="gram_quarters",
    )(own, *row_parts)


def factor_block(matrix):
    side = matrix.shape[0]
    tiles = side // 8
    v = [matrix[8 * t : 8 * t + 8, :] for t in range(tiles)]
    lane = lax.broadcasted_iota(jnp.int32, (8, side), 1)
    sub = lax.broadcasted_iota(jnp.int32, (8, side), 0)
    inverse = []
    log_row = jnp.zeros((8, side), jnp.float32)
    for t0 in range(tiles):
        base = 8 * t0
        panel = v[t0]
        in_panel = (lane >= base) & (lane < base + 8)
        column = [jnp.broadcast_to(panel[:, base + q : base + q + 1], (8, side)) for q in range(8)]
        splat = [
            [jnp.broadcast_to(column[p][q : q + 1, :], (8, side)) for p in range(q + 1)]
            for q in range(8)
        ]
        recip, lower = [], [[None] * 8 for _ in range(8)]
        for p in range(8):
            recip.append(1.0 / splat[p][p])
            for q in range(p + 1, 8):
                lower[q][p] = splat[q][p] * recip[p]
            for q in range(p + 1, 8):
                for r in range(p + 1, q + 1):
                    splat[q][r] = splat[q][r] - lower[q][p] * splat[r][p]
        rows = []
        for q in range(8):
            own = jnp.broadcast_to(panel[q : q + 1, :], (8, side))
            own = jnp.where(in_panel, (lane == base + q).astype(jnp.float32), own)
            for p in range(q):
                own = own - lower[q][p] * rows[p]
            rows.append(own)
        for t in range(t0 + 1, tiles):
            reduced = []
            fresh = jnp.where(in_panel, 0.0, v[t])
            for p in range(8):
                mine = jnp.broadcast_to(v[t][:, base + p : base + p + 1], (8, side))
                for r in range(p):
                    mine = mine - lower[p][r] * reduced[r]
                reduced.append(mine)
                fresh = fresh - (mine * recip[p]) * rows[p]
            v[t] = fresh
        done, pivots = rows[0], splat[0][0]
        for q in range(1, 8):
            done = jnp.where(sub == q, rows[q], done)
            pivots = jnp.where(sub == q, splat[q][q], pivots)
        inverse.append(jnp.where(lane <= sub + base, done * lax.rsqrt(pivots), 0.0))
        log_row = log_row + jnp.where(lane == sub + base, 0.5 * jnp.log(pivots), 0.0)
    return jnp.concatenate(inverse, axis=0), jnp.sum(log_row, axis=0, keepdims=True)


def factor_kernel(scale, own_ref, *refs):
    inv_ref, log_ref, m_ref, z_ref = refs[-4:]
    parts = m_ref.shape[0]
    side = m_ref.shape[2]
    half = side // 2
    for a in range(parts):
        for b in range(a):
            m_ref[a, b] = jnp.zeros((side, side), jnp.float32)
    for k in range(parts):
        device = lax.rem(own_ref[0] + parts - k, parts)
        after = lax.rem(device + 1, parts)
        m_ref[device, device] = refs[k][:side, :] * scale
        second = refs[k][side : 2 * side, :] * scale
        m_ref[jnp.minimum(device, after), jnp.maximum(device, after)] = jnp.where(
            after < device, second.T, second
        )
        low = lax.rem(device, 2)
        m_ref[low, low + 2, pl.ds(pl.multiple_of(device // 2 * half, half), half), :] = (
            refs[k][2 * side :, :] * scale
        )
    sub = lax.broadcasted_iota(jnp.int32, (side, side), 0)
    lane = lax.broadcasted_iota(jnp.int32, (side, side), 1)
    eye = (sub == lane).astype(jnp.float32)

    @pl.loop(0, parts)
    def _(k):
        inverse, logs = factor_block(m_ref[k, k])
        log_ref[pl.ds(k, 1), :] = logs
        for b in range(parts):
            block = jnp.where(k == b, eye, m_ref[k, b])
            z_ref[b] = split_dot(inverse, block, 1, 0)
        for b in range(parts):
            inv_ref[k, b] = jnp.where(b <= k, z_ref[b], 0.0).astype(jnp.bfloat16)
        for a in range(1, parts):

            @pl.when(a > k)
            def _():
                for b in range(parts):
                    change = split_dot(z_ref[a], z_ref[b], 0, 0)
                    m_ref[a, b] = jnp.where(k == b, 0.0, m_ref[a, b]) - change


def cholesky_parts(own, quarters, unit_total):
    parts = len(quarters)
    side = quarters[0].shape[1]
    vmem = pl.BlockSpec(memory_space=pltpu.VMEM)
    return pl.pallas_call(
        functools.partial(factor_kernel, 1.0 / unit_total),
        in_specs=[pl.BlockSpec(memory_space=pltpu.SMEM)] + [vmem] * parts,
        out_specs=[vmem, vmem],
        out_shape=[
            jax.ShapeDtypeStruct((parts, parts, side, side), jnp.bfloat16),
            jax.ShapeDtypeStruct((parts, side), jnp.float32),
        ],
        scratch_shapes=[
            pltpu.VMEM((parts, parts, side, side), jnp.float32),
            pltpu.VMEM((parts, side, side), jnp.float32),
        ],
        compiler_params=pltpu.CompilerParams(vmem_limit_bytes=16 * MIB),
        cost_estimate=pl.CostEstimate(
            flops=200_000_000, bytes_accessed=2 * MIB, transcendentals=100_000
        ),
        name="factor",
    )(own, *quarters)


def renew_kernel(own_ref, *refs):
    s_refs, (inv_ref, out_ref) = refs[:-2], refs[-2:]
    own = own_ref[0]
    parts = len(s_refs)
    total = None
    for k in range(parts):
        term = lax.dot_general(
            s_refs[k][...],
            inv_ref[own, lax.rem(own + parts - k, parts)],
            (((1,), (1,)), ((), ())),
            preferred_element_type=jnp.float32,
        )
        total = term if total is None else total + term
    out_ref[...] = total.astype(jnp.bfloat16)


def renew(own, vectors, inverse):
    parts = len(vectors)
    rows, width = vectors[0].shape
    side = inverse.shape[-1]
    chunk = rows // 4
    rows_spec = pl.BlockSpec((chunk, width), lambda i, *_: (i, 0))
    return pl.pallas_call(
        renew_kernel,
        grid_spec=pltpu.PrefetchScalarGridSpec(
            num_scalar_prefetch=1,
            grid=(rows // chunk,),
            in_specs=[rows_spec] * parts
            + [pl.BlockSpec((parts, parts, side, side), lambda i, *_: (0, 0, 0, 0))],
            out_specs=pl.BlockSpec((chunk, side), lambda i, *_: (i, 0)),
        ),
        out_shape=jax.ShapeDtypeStruct((rows, side), jnp.bfloat16),
        compiler_params=pltpu.CompilerParams(vmem_limit_bytes=16 * MIB),
        cost_estimate=pl.CostEstimate(
            flops=2 * parts * rows * width * side, bytes_accessed=6 * MIB, transcendentals=0
        ),
        name="renew",
    )(own, *vectors, inverse)


def around(parts, step):
    return [(i, (i + step) % parts) for i in range(parts)]


def onward(parts, step):
    return [(i, i + step) for i in range(parts - step)]


def body(
    tangents,
    state,
    gain,
    local_w,
    local_row,
    local_col,
    remote_w,
    remote_row,
    remote_owner,
    remote_offset,
):
    rows_dev, width = tangents.shape
    side = local_w.shape[1]
    block_rows = rows_dev // side
    units = lax.axis_size("unit")
    parts = lax.axis_size("vec")
    unit_total = float(rows_dev * units)

    assert side == 2 * units and units <= 256 and block_rows <= 256
    blocks = tangents.reshape(block_rows, side, width)
    ask = jnp.concatenate([remote_owner[:, 0], remote_offset]).astype(jnp.bfloat16)
    far_count = remote_offset.shape[0]
    pieces, spread = spread_pieces(state, gain, blocks, ask.reshape(1, width), units)
    table = lax.all_to_all(spread, "unit", 0, 0, tiled=True)
    asked = table[:, 2 * block_rows, :].astype(jnp.float32)
    index = asked[:, :far_count] * block_rows + asked[:, far_count:]
    chosen = pick_rows(index, table, block_rows)
    arrived = lax.all_to_all(chosen, "unit", 0, 0, tiled=True)

    own = lax.axis_index("vec").astype(jnp.int32).reshape(1)
    steps = (2, 1, 3)
    assert parts == 4
    acc = local_product(local_row, local_col, local_w, pieces, blocks)
    stepped, *outgoing = far_product(own, remote_row, remote_w, acc, arrived, parts)

    row_parts = [outgoing[0]] + [None] * 3
    for k in steps:
        row_parts[k] = lax.ppermute(outgoing[k], "vec", around(parts, k))
    quarters = gram_quarters(own, [part.reshape(rows_dev // parts, width) for part in row_parts])
    mine = quarters[0]
    for k in steps:
        mine = mine + lax.ppermute(quarters[k], "vec", around(parts, k))

    late, mine = lax.optimization_barrier((stepped.reshape(rows_dev, width), mine))
    vectors = [late] + [None] * 3
    for k in steps:
        vectors[k] = lax.ppermute(late, "vec", onward(parts, k))

    share = mine.size // units
    by_unit = lax.all_to_all(mine.reshape(units, 1, share), "unit", 0, 0, tiled=True)
    summed = jnp.sum(by_unit, axis=0, keepdims=True)
    spread_sum = jnp.broadcast_to(summed, (units, 1, share))
    quarter = lax.all_to_all(spread_sum, "unit", 0, 0, tiled=True).reshape(mine.shape)
    gathered = [quarter] + [None] * 3
    for k in steps:
        gathered[k] = lax.ppermute(quarter, "vec", around(parts, k))

    inverse, logs = cholesky_parts(own, gathered, unit_total)
    renewed = renew(own, vectors, inverse)
    return (renewed, logs.reshape(parts * width))


def solution(mesh):
    placed = (
        P("unit", "vec"),
        P("unit"),
        P("unit"),
        P("unit", None, None),
        P("unit"),
        P("unit"),
        P("unit", None, None),
        P("unit"),
        P("unit", None),
        P("unit"),
    )
    return jax.shard_map(
        body, mesh=mesh, in_specs=placed, out_specs=(P("unit", "vec"), P()), check_vma=False
    )
```

```python
import functools

import jax
import jax.numpy as jnp
from jax import lax
from jax.experimental import pallas as pl
from jax.experimental.pallas import tpu as pltpu
from jax.sharding import PartitionSpec as P

time_step = 0.5
HIGHEST = lax.Precision.HIGHEST
MIB = 1024 * 1024


def split_dot(left, right, left_dim, right_dim):
    return lax.dot_general(
        left,
        right,
        (((left_dim,), (right_dim,)), ((), ())),
        precision=HIGHEST,
        preferred_element_type=jnp.float32,
    )


def local_kernel(row_ref, col_ref, w_ref, x_ref, t_ref, acc_ref):
    step = pl.program_id(0)
    count = w_ref.shape[0]

    @pl.when(step == 0)
    def _():
        acc_ref[...] = t_ref[...].astype(jnp.float32)

    @pl.loop(0, count // 8)
    def _(group):
        for inner in range(8):
            block = group * 8 + inner
            row = row_ref[step * count + block]
            col = col_ref[step * count + block]
            acc_ref[row] += jnp.dot(w_ref[block], x_ref[col], preferred_element_type=jnp.float32)


def local_product(local_row, local_col, local_w, pieces, tangents):
    count, side, _ = local_w.shape
    block_rows, _, width = pieces.shape
    chunk = 32
    whole = lambda i, *_: (0, 0, 0)
    return pl.pallas_call(
        local_kernel,
        grid_spec=pltpu.PrefetchScalarGridSpec(
            num_scalar_prefetch=2,
            grid=(count // chunk,),
            in_specs=[
                pl.BlockSpec((chunk, side, side), lambda i, *_: (i, 0, 0)),
                pl.BlockSpec((block_rows, side, width), whole),
                pl.BlockSpec((block_rows, side, width), whole),
            ],
            out_specs=pl.BlockSpec((block_rows, side, width), whole),
        ),
        out_shape=pltpu.HBM((block_rows, side, width), jnp.float32),
        compiler_params=pltpu.CompilerParams(vmem_limit_bytes=16 * MIB),
        cost_estimate=pl.CostEstimate(
            flops=2 * count * side * side * width, bytes_accessed=14 * MIB, transcendentals=0
        ),
        name="local_blocks",
    )(local_row, local_col, local_w, pieces, tangents)


def column_of(row, side):
    return jnp.broadcast_to(row, (side, side)).T


def spread_kernel(*refs):
    sources, (pieces_ref, spread_ref), targets, sems = refs[:5], refs[5:7], refs[7:12], refs[12]
    owner_ref, offset_ref, state_ref, gain_ref, t_ref = targets
    copies = [
        pltpu.make_async_copy(source, target, sems.at[i])
        for i, (source, target) in enumerate(zip(sources, targets))
    ]
    for copy in copies:
        copy.start()
    block_rows, side, width = t_ref.shape
    half = side // 2
    units, rows, _ = spread_ref.shape
    extra = rows - 2 * block_rows
    copies[0].wait()
    copies[1].wait()
    ask = jnp.concatenate([owner_ref[...], offset_ref[...]], axis=1).astype(jnp.float32)
    spread_ref[:, 2 * block_rows :, :] = jnp.broadcast_to(
        ask.reshape(1, 1, width), (units, extra, width)
    ).astype(jnp.bfloat16)
    copies[2].wait()
    copies[3].wait()
    gain = gain_ref[...]
    slopes = gain * (1.0 - jnp.tanh(gain * state_ref[...]) ** 2)
    copies[4].wait()
    for p in range(block_rows):
        slope = column_of(slopes[p : p + 1, :], side)
        pieces_ref[p] = (slope * t_ref[p].astype(jnp.float32)).astype(jnp.bfloat16)
    for h in range(2):
        for g in range(block_rows // 16):
            group = pieces_ref[16 * g : 16 * g + 16, h * half : (h + 1) * half, :]
            at = h * block_rows + 16 * g
            spread_ref[:, at : at + 16, :] = jnp.swapaxes(group, 0, 1)


def in_hbm(*arrays):
    return [pltpu.with_memory_space_constraint(array, pltpu.HBM) for array in arrays]


def spread_pieces(state, gain, blocks, owner, offset, units):
    block_rows, side, width = blocks.shape
    rows = 2 * block_rows + 8
    count = offset.shape[0]
    vmem = pl.BlockSpec(memory_space=pltpu.VMEM)
    hbm = pl.BlockSpec(memory_space=pltpu.HBM)
    return pl.pallas_call(
        spread_kernel,
        in_specs=[hbm] * 5,
        out_specs=[vmem] * 2,
        out_shape=[
            jax.ShapeDtypeStruct((block_rows, side, width), jnp.bfloat16),
            jax.ShapeDtypeStruct((units, rows, width), jnp.bfloat16),
        ],
        scratch_shapes=[
            pltpu.VMEM((1, count), jnp.int32),
            pltpu.VMEM((1, count), jnp.int32),
            pltpu.VMEM((block_rows, side), jnp.float32),
            pltpu.VMEM((block_rows, side), jnp.float32),
            pltpu.VMEM((block_rows, side, width), jnp.bfloat16),
            pltpu.SemaphoreType.DMA((5,)),
        ],
        compiler_params=pltpu.CompilerParams(vmem_limit_bytes=16 * MIB),
        cost_estimate=pl.CostEstimate(
            flops=4 * MIB, bytes_accessed=4 * MIB, transcendentals=block_rows * side
        ),
        name="spread_pieces",
    )(
        *in_hbm(
            owner.reshape(1, count),
            offset.reshape(1, count),
            state.reshape(block_rows, side),
            gain.reshape(block_rows, side),
            blocks,
        )
    )


def pick_kernel(block_rows, index_ref, table_ref, out_ref):
    shards, rows, width = out_ref.shape
    owners = table_ref.shape[0]
    depth = owners * block_rows
    table = jnp.concatenate(
        [
            table_ref[:, h * block_rows : (h + 1) * block_rows, :].reshape(depth, width)
            for h in range(2)
        ],
        axis=1,
    )
    index = jnp.concatenate(
        [column_of(index_ref[0, g : g + 1, :], width) for g in range(index_ref.shape[1])], axis=0
    ).astype(jnp.int32)
    lane = lax.broadcasted_iota(jnp.int32, index.shape, 1)
    hot = jnp.concatenate(
        [(index == lane + width * k).astype(jnp.bfloat16) for k in range(depth // width)], axis=1
    )
    found = jnp.dot(hot, table, preferred_element_type=jnp.float32).astype(jnp.bfloat16)
    found = found.reshape(shards, rows // 2, 2 * width)
    out_ref[:, : rows // 2, :] = found[:, :, :width]
    out_ref[:, rows // 2 :, :] = found[:, :, width:]


def pick_rows(index, table, block_rows):
    units, far_count = index.shape
    width = table.shape[-1]
    steps = 4
    lines = units * far_count // width // steps
    return pl.pallas_call(
        functools.partial(pick_kernel, block_rows),
        grid=(steps,),
        in_specs=[
            pl.BlockSpec((1, lines, width), lambda i: (i, 0, 0)),
            pl.BlockSpec(table.shape, lambda i: (0, 0, 0)),
        ],
        out_specs=pl.BlockSpec((units // steps, 2 * far_count, width), lambda i: (i, 0, 0)),
        out_shape=pltpu.HBM((units, 2 * far_count, width), jnp.bfloat16),
        compiler_params=pltpu.CompilerParams(vmem_limit_bytes=32 * MIB),
        cost_estimate=pl.CostEstimate(
            flops=4_000_000_000, bytes_accessed=4 * MIB, transcendentals=0
        ),
        name="pick_rows",
    )(index.reshape(steps, lines, width), table)


def far_kernel(own_ref, row_ref, w_hbm, acc_hbm, arrived_ref, *rest):
    part_refs, (far_ref, acc_ref, w_ref, x_ref, sems) = rest[:-5], rest[-5:]
    count = w_ref.shape[0]
    units = arrived_ref.shape[0]
    groups = count // 16
    w_copies = [
        pltpu.make_async_copy(
            w_hbm.at[pl.ds(16 * g, 16)], w_ref.at[pl.ds(16 * g, 16)], sems.at[g]
        )
        for g in range(groups)
    ]
    acc_copy = pltpu.make_async_copy(acc_hbm, acc_ref, sems.at[groups])
    for copy in w_copies:
        copy.start()
    acc_copy.start()
    far_ref[...] = jnp.zeros_like(far_ref)
    for g in range(groups):
        for h in range(2):
            at = h * count + 16 * g
            x_ref[16 * g : 16 * g + 16, h * units : (h + 1) * units, :] = jnp.swapaxes(
                arrived_ref[:, at : at + 16, :], 0, 1
            )
    for g in range(groups):
        w_copies[g].wait()
        for inner in range(16):
            block = 16 * g + inner
            row = row_ref[block]
            far_ref[row] += jnp.dot(w_ref[block], x_ref[block], preferred_element_type=jnp.float32)
    acc_copy.wait()
    parts = len(part_refs)
    for k in range(parts):
        share = part_refs[k].shape[0]
        here = pl.ds(lax.rem(own_ref[0] + k, parts) * share, share)
        part_refs[k][...] = (time_step * (acc_ref[here] + far_ref[here])).astype(jnp.bfloat16)


def far_product(own, remote_row, remote_w, acc, arrived, parts):
    count, side, _ = remote_w.shape
    block_rows, _, width = acc.shape
    vmem = pl.BlockSpec(memory_space=pltpu.VMEM)
    smem = pl.BlockSpec(memory_space=pltpu.SMEM)
    hbm = pl.BlockSpec(memory_space=pltpu.HBM)
    return pl.pallas_call(
        far_kernel,
        in_specs=[smem, smem, hbm, hbm, vmem],
        out_specs=[vmem] * parts,
        out_shape=[jax.ShapeDtypeStruct((block_rows // parts, side, width), jnp.bfloat16)] * parts,
        scratch_shapes=[
            pltpu.VMEM((block_rows, side, width), jnp.float32),
            pltpu.VMEM((block_rows, side, width), jnp.float32),
            pltpu.VMEM((count, side, side), jnp.bfloat16),
            pltpu.VMEM((count, side, width), jnp.bfloat16),
            pltpu.SemaphoreType.DMA((count // 16 + 1,)),
        ],
        compiler_params=pltpu.CompilerParams(vmem_limit_bytes=24 * MIB),
        cost_estimate=pl.CostEstimate(
            flops=2 * count * side * side * width, bytes_accessed=8 * MIB, transcendentals=0
        ),
        name="far_blocks",
    )(own, remote_row, *in_hbm(remote_w, acc), arrived)


def cross(left, right):
    return lax.dot_general(
        left, right, (((0,), (0,)), ((), ())), preferred_element_type=jnp.float32
    )


def gram_kernel(own_ref, *refs):
    parts = len(refs) // 2
    x_refs, out_refs = refs[:parts], refs[parts:]
    side = x_refs[0].shape[1]
    half = side // 2
    for k in range(parts):
        device = lax.rem(own_ref[0] + k, parts)
        here, after, across = (x_refs[(-k - step) % parts][...] for step in (0, 1, 2))
        products = cross(here, jnp.concatenate([here, after, across], axis=1))
        out_refs[k][:side, :] = products[:, :side]
        out_refs[k][side : 2 * side, :] = products[:, side : 2 * side]
        last = products[:, 2 * side :]
        out_refs[k][2 * side :, :] = jnp.where(device < 2, last[:half], last.T[half:])


def gram_quarters(own, row_parts):
    parts = len(row_parts)
    rows, side = row_parts[0].shape
    vmem = pl.BlockSpec(memory_space=pltpu.VMEM)
    return pl.pallas_call(
        gram_kernel,
        in_specs=[pl.BlockSpec(memory_space=pltpu.SMEM)] + [vmem] * parts,
        out_specs=[vmem] * parts,
        out_shape=[jax.ShapeDtypeStruct((2 * side + side // 2, side), jnp.float32)] * parts,
        compiler_params=pltpu.CompilerParams(vmem_limit_bytes=16 * MIB),
        cost_estimate=pl.CostEstimate(
            flops=6 * parts * rows * side * side, bytes_accessed=2 * MIB, transcendentals=0
        ),
        name="gram_quarters",
    )(own, *row_parts)


def factor_block(matrix):
    side = matrix.shape[0]
    tiles = side // 8
    v = [matrix[8 * t : 8 * t + 8, :] for t in range(tiles)]
    lane = lax.broadcasted_iota(jnp.int32, (8, side), 1)
    sub = lax.broadcasted_iota(jnp.int32, (8, side), 0)
    inverse = []
    log_row = jnp.zeros((8, side), jnp.float32)
    for t0 in range(tiles):
        base = 8 * t0
        panel = v[t0]
        in_panel = (lane >= base) & (lane < base + 8)
        column = [jnp.broadcast_to(panel[:, base + q : base + q + 1], (8, side)) for q in range(8)]
        splat = [
            [jnp.broadcast_to(column[p][q : q + 1, :], (8, side)) for p in range(q + 1)]
            for q in range(8)
        ]
        recip, lower = [], [[None] * 8 for _ in range(8)]
        for p in range(8):
            recip.append(1.0 / splat[p][p])
            for q in range(p + 1, 8):
                lower[q][p] = splat[q][p] * recip[p]
            for q in range(p + 1, 8):
                for r in range(p + 1, q + 1):
                    splat[q][r] = splat[q][r] - lower[q][p] * splat[r][p]
        rows = []
        for q in range(8):
            own = jnp.broadcast_to(panel[q : q + 1, :], (8, side))
            own = jnp.where(in_panel, (lane == base + q).astype(jnp.float32), own)
            for p in range(q):
                own = own - lower[q][p] * rows[p]
            rows.append(own)
        for t in range(t0 + 1, tiles):
            reduced = []
            fresh = jnp.where(in_panel, 0.0, v[t])
            for p in range(8):
                mine = jnp.broadcast_to(v[t][:, base + p : base + p + 1], (8, side))
                for r in range(p):
                    mine = mine - lower[p][r] * reduced[r]
                reduced.append(mine)
                fresh = fresh - (mine * recip[p]) * rows[p]
            v[t] = fresh
        done, pivots = rows[0], splat[0][0]
        for q in range(1, 8):
            done = jnp.where(sub == q, rows[q], done)
            pivots = jnp.where(sub == q, splat[q][q], pivots)
        inverse.append(jnp.where(lane <= sub + base, done * lax.rsqrt(pivots), 0.0))
        log_row = log_row + jnp.where(lane == sub + base, 0.5 * jnp.log(pivots), 0.0)
    return jnp.concatenate(inverse, axis=0), jnp.sum(log_row, axis=0, keepdims=True)


def factor_kernel(scale, own_ref, *refs):
    inv_ref, log_ref, m_ref, z_ref = refs[-4:]
    parts = m_ref.shape[0]
    side = m_ref.shape[2]
    half = side // 2
    for a in range(parts):
        for b in range(a):
            m_ref[a, b] = jnp.zeros((side, side), jnp.float32)
    for k in range(parts):
        device = lax.rem(own_ref[0] + parts - k, parts)
        after = lax.rem(device + 1, parts)
        m_ref[device, device] = refs[k][:side, :] * scale
        second = refs[k][side : 2 * side, :] * scale
        m_ref[jnp.minimum(device, after), jnp.maximum(device, after)] = jnp.where(
            after < device, second.T, second
        )
        low = lax.rem(device, 2)
        m_ref[low, low + 2, pl.ds(pl.multiple_of(device // 2 * half, half), half), :] = (
            refs[k][2 * side :, :] * scale
        )
    sub = lax.broadcasted_iota(jnp.int32, (side, side), 0)
    lane = lax.broadcasted_iota(jnp.int32, (side, side), 1)
    eye = (sub == lane).astype(jnp.float32)

    @pl.loop(0, parts)
    def _(k):
        inverse, logs = factor_block(m_ref[k, k])
        log_ref[pl.ds(k, 1), :] = logs
        for b in range(parts):
            block = jnp.where(k == b, eye, m_ref[k, b])
            z_ref[b] = split_dot(inverse, block, 1, 0)
        for b in range(parts):
            inv_ref[k, b] = jnp.where(b <= k, z_ref[b], 0.0).astype(jnp.bfloat16)
        for a in range(1, parts):

            @pl.when(a > k)
            def _():
                for b in range(parts):
                    change = split_dot(z_ref[a], z_ref[b], 0, 0)
                    m_ref[a, b] = jnp.where(k == b, 0.0, m_ref[a, b]) - change


def cholesky_parts(own, quarters, unit_total):
    parts = len(quarters)
    side = quarters[0].shape[1]
    vmem = pl.BlockSpec(memory_space=pltpu.VMEM)
    return pl.pallas_call(
        functools.partial(factor_kernel, 1.0 / unit_total),
        in_specs=[pl.BlockSpec(memory_space=pltpu.SMEM)] + [vmem] * parts,
        out_specs=[vmem, vmem],
        out_shape=[
            jax.ShapeDtypeStruct((parts, parts, side, side), jnp.bfloat16),
            jax.ShapeDtypeStruct((parts, side), jnp.float32),
        ],
        scratch_shapes=[
            pltpu.VMEM((parts, parts, side, side), jnp.float32),
            pltpu.VMEM((parts, side, side), jnp.float32),
        ],
        compiler_params=pltpu.CompilerParams(vmem_limit_bytes=16 * MIB),
        cost_estimate=pl.CostEstimate(
            flops=200_000_000, bytes_accessed=2 * MIB, transcendentals=100_000
        ),
        name="factor",
    )(own, *quarters)


def renew_kernel(own_ref, *refs):
    x_refs, (inv_ref, out_ref) = refs[:-2], refs[-2:]
    own = own_ref[0]
    parts = len(x_refs)
    for b in range(parts):
        total = None
        for k in range(parts):
            term = lax.dot_general(
                x_refs[k][...],
                inv_ref[b, lax.rem(own + parts - k, parts)],
                (((1,), (1,)), ((), ())),
                preferred_element_type=jnp.float32,
            )
            total = term if total is None else total + term
        out_ref[b] = total.astype(jnp.bfloat16)


def renew(own, row_parts, inverse):
    parts = len(row_parts)
    rows, width = row_parts[0].shape
    side = inverse.shape[-1]
    vmem = pl.BlockSpec(memory_space=pltpu.VMEM)
    return pl.pallas_call(
        renew_kernel,
        in_specs=[pl.BlockSpec(memory_space=pltpu.SMEM)] + [vmem] * (parts + 1),
        out_specs=vmem,
        out_shape=jax.ShapeDtypeStruct((parts, rows, side), jnp.bfloat16),
        compiler_params=pltpu.CompilerParams(vmem_limit_bytes=16 * MIB),
        cost_estimate=pl.CostEstimate(
            flops=2 * parts * parts * rows * width * side,
            bytes_accessed=2 * MIB,
            transcendentals=0,
        ),
        name="renew",
    )(own, *row_parts, inverse)


def around(parts, step):
    return [(i, (i + step) % parts) for i in range(parts)]


def body(
    tangents,
    state,
    gain,
    local_w,
    local_row,
    local_col,
    remote_w,
    remote_row,
    remote_owner,
    remote_offset,
):
    rows_dev, width = tangents.shape
    side = local_w.shape[1]
    block_rows = rows_dev // side
    units = lax.axis_size("unit")
    parts = lax.axis_size("vec")
    unit_total = float(rows_dev * units)

    assert side == 2 * units and units <= 256 and block_rows <= 256
    blocks = tangents.reshape(block_rows, side, width)
    far_count = remote_offset.shape[0]
    pieces, spread = spread_pieces(state, gain, blocks, remote_owner, remote_offset, units)
    table = lax.all_to_all(spread, "unit", 0, 0, tiled=True)
    asked = table[:, 2 * block_rows, :].astype(jnp.float32)
    index = asked[:, :far_count] * block_rows + asked[:, far_count:]
    chosen = pick_rows(index, table, block_rows)
    arrived = lax.all_to_all(chosen, "unit", 0, 0, tiled=True)

    own = lax.axis_index("vec").astype(jnp.int32).reshape(1)
    steps = (2, 1, 3)
    assert parts == 4
    acc = local_product(local_row, local_col, local_w, pieces, blocks)
    outgoing = far_product(own, remote_row, remote_w, acc, arrived, parts)

    row_parts = [outgoing[0]] + [None] * 3
    for k in steps:
        row_parts[k] = lax.ppermute(outgoing[k], "vec", around(parts, k))
    row_parts = [part.reshape(rows_dev // parts, width) for part in row_parts]
    quarters = gram_quarters(own, row_parts)
    mine = quarters[0]
    for k in steps:
        mine = mine + lax.ppermute(quarters[k], "vec", around(parts, k))

    share = mine.size // units
    by_unit = lax.all_to_all(mine.reshape(units, 1, share), "unit", 0, 0, tiled=True)
    summed = jnp.sum(by_unit, axis=0, keepdims=True)
    spread_sum = jnp.broadcast_to(summed, (units, 1, share))
    quarter = lax.all_to_all(spread_sum, "unit", 0, 0, tiled=True).reshape(mine.shape)
    gathered = [quarter] + [None] * 3
    for k in steps:
        gathered[k] = lax.ppermute(quarter, "vec", around(parts, k))

    inverse, logs = cholesky_parts(own, gathered, unit_total)
    renewed = lax.all_to_all(renew(own, row_parts, inverse), "vec", 0, 0, tiled=True)
    return (renewed.reshape(rows_dev, width), logs.reshape(parts * width))


def solution(mesh):
    placed = (
        P("unit", "vec"),
        P("unit"),
        P("unit"),
        P("unit", None, None),
        P("unit"),
        P("unit"),
        P("unit", None, None),
        P("unit"),
        P("unit", None),
        P("unit"),
    )
    return jax.shard_map(
        body, mesh=mesh, in_specs=placed, out_specs=(P("unit", "vec"), P()), check_vma=False
    )
```

```python
import functools

import jax
import jax.numpy as jnp
from jax import lax
from jax.experimental import pallas as pl
from jax.experimental.pallas import tpu as pltpu
from jax.sharding import PartitionSpec as P

time_step = 0.5
HIGHEST = lax.Precision.HIGHEST
MIB = 1024 * 1024


def split_dot(left, right, left_dim, right_dim):
    return lax.dot_general(
        left,
        right,
        (((left_dim,), (right_dim,)), ((), ())),
        precision=HIGHEST,
        preferred_element_type=jnp.float32,
    )


def local_kernel(row_ref, col_ref, w_ref, x_ref, t_ref, acc_ref):
    step = pl.program_id(0)
    count = w_ref.shape[0]

    @pl.when(step == 0)
    def _():
        acc_ref[...] = t_ref[...].astype(jnp.float32)

    @pl.loop(0, count // 8)
    def _(group):
        for inner in range(8):
            block = group * 8 + inner
            row = row_ref[step * count + block]
            col = col_ref[step * count + block]
            acc_ref[row] += jnp.dot(w_ref[block], x_ref[col], preferred_element_type=jnp.float32)


def local_product(local_row, local_col, local_w, pieces, tangents):
    count, side, _ = local_w.shape
    block_rows, _, width = pieces.shape
    chunk = 32
    whole = lambda i, *_: (0, 0, 0)
    return pl.pallas_call(
        local_kernel,
        grid_spec=pltpu.PrefetchScalarGridSpec(
            num_scalar_prefetch=2,
            grid=(count // chunk,),
            in_specs=[
                pl.BlockSpec((chunk, side, side), lambda i, *_: (i, 0, 0)),
                pl.BlockSpec((block_rows, side, width), whole),
                pl.BlockSpec((block_rows, side, width), whole),
            ],
            out_specs=pl.BlockSpec((block_rows, side, width), whole),
        ),
        out_shape=pltpu.HBM((block_rows, side, width), jnp.float32),
        compiler_params=pltpu.CompilerParams(vmem_limit_bytes=16 * MIB),
        cost_estimate=pl.CostEstimate(
            flops=2 * count * side * side * width, bytes_accessed=14 * MIB, transcendentals=0
        ),
        name="local_blocks",
    )(local_row, local_col, local_w, pieces, tangents)


def column_of(row, side):
    return jnp.broadcast_to(row, (side, side)).T


def spread_kernel(*refs):
    sources, (pieces_ref, spread_ref), targets, sems = refs[:5], refs[5:7], refs[7:12], refs[12]
    owner_ref, offset_ref, state_ref, gain_ref, t_ref = targets
    copies = [
        pltpu.make_async_copy(source, target, sems.at[i])
        for i, (source, target) in enumerate(zip(sources, targets))
    ]
    for copy in copies:
        copy.start()
    block_rows, side, width = t_ref.shape
    half = side // 2
    units, rows, _ = spread_ref.shape
    extra = rows - 2 * block_rows
    copies[0].wait()
    copies[1].wait()
    ask = jnp.concatenate([owner_ref[...], offset_ref[...]], axis=1).astype(jnp.float32)
    spread_ref[:, 2 * block_rows :, :] = jnp.broadcast_to(
        ask.reshape(1, 1, width), (units, extra, width)
    ).astype(jnp.bfloat16)
    copies[2].wait()
    copies[3].wait()
    gain = gain_ref[...]
    slopes = gain * (1.0 - jnp.tanh(gain * state_ref[...]) ** 2)
    copies[4].wait()
    for p in range(block_rows):
        slope = column_of(slopes[p : p + 1, :], side)
        pieces_ref[p] = (slope * t_ref[p].astype(jnp.float32)).astype(jnp.bfloat16)
    for h in range(2):
        for g in range(block_rows // 16):
            group = pieces_ref[16 * g : 16 * g + 16, h * half : (h + 1) * half, :]
            at = h * block_rows + 16 * g
            spread_ref[:, at : at + 16, :] = jnp.swapaxes(group, 0, 1)


def in_hbm(*arrays):
    return [pltpu.with_memory_space_constraint(array, pltpu.HBM) for array in arrays]


def spread_pieces(state, gain, blocks, owner, offset, units):
    block_rows, side, width = blocks.shape
    rows = 2 * block_rows + 8
    count = offset.shape[0]
    vmem = pl.BlockSpec(memory_space=pltpu.VMEM)
    hbm = pl.BlockSpec(memory_space=pltpu.HBM)
    return pl.pallas_call(
        spread_kernel,
        in_specs=[hbm] * 5,
        out_specs=[vmem] * 2,
        out_shape=[
            jax.ShapeDtypeStruct((block_rows, side, width), jnp.bfloat16),
            jax.ShapeDtypeStruct((units, rows, width), jnp.bfloat16),
        ],
        scratch_shapes=[
            pltpu.VMEM((1, count), jnp.int32),
            pltpu.VMEM((1, count), jnp.int32),
            pltpu.VMEM((block_rows, side), jnp.float32),
            pltpu.VMEM((block_rows, side), jnp.float32),
            pltpu.VMEM((block_rows, side, width), jnp.bfloat16),
            pltpu.SemaphoreType.DMA((5,)),
        ],
        compiler_params=pltpu.CompilerParams(vmem_limit_bytes=16 * MIB),
        cost_estimate=pl.CostEstimate(
            flops=4 * MIB, bytes_accessed=4 * MIB, transcendentals=block_rows * side
        ),
        name="spread_pieces",
    )(
        *in_hbm(
            owner.reshape(1, count),
            offset.reshape(1, count),
            state.reshape(block_rows, side),
            gain.reshape(block_rows, side),
            blocks,
        )
    )


def pick_kernel(block_rows, index_ref, table_ref, out_ref):
    shards, rows, width = out_ref.shape
    owners = table_ref.shape[0]
    depth = owners * block_rows
    table = jnp.concatenate(
        [
            table_ref[:, h * block_rows : (h + 1) * block_rows, :].reshape(depth, width)
            for h in range(2)
        ],
        axis=1,
    )
    index = jnp.concatenate(
        [column_of(index_ref[0, g : g + 1, :], width) for g in range(index_ref.shape[1])], axis=0
    ).astype(jnp.int32)
    lane = lax.broadcasted_iota(jnp.int32, index.shape, 1)
    hot = jnp.concatenate(
        [(index == lane + width * k).astype(jnp.bfloat16) for k in range(depth // width)], axis=1
    )
    found = jnp.dot(hot, table, preferred_element_type=jnp.float32).astype(jnp.bfloat16)
    found = found.reshape(shards, rows // 2, 2 * width)
    out_ref[:, : rows // 2, :] = found[:, :, :width]
    out_ref[:, rows // 2 :, :] = found[:, :, width:]


def pick_rows(index, table, block_rows):
    units, far_count = index.shape
    width = table.shape[-1]
    steps = 4
    lines = units * far_count // width // steps
    return pl.pallas_call(
        functools.partial(pick_kernel, block_rows),
        grid=(steps,),
        in_specs=[
            pl.BlockSpec((1, lines, width), lambda i: (i, 0, 0)),
            pl.BlockSpec(table.shape, lambda i: (0, 0, 0)),
        ],
        out_specs=pl.BlockSpec((units // steps, 2 * far_count, width), lambda i: (i, 0, 0)),
        out_shape=pltpu.HBM((units, 2 * far_count, width), jnp.bfloat16),
        compiler_params=pltpu.CompilerParams(vmem_limit_bytes=32 * MIB),
        cost_estimate=pl.CostEstimate(
            flops=4_000_000_000, bytes_accessed=4 * MIB, transcendentals=0
        ),
        name="pick_rows",
    )(index.reshape(steps, lines, width), table)


def far_kernel(own_ref, row_ref, w_hbm, acc_hbm, arrived_ref, *rest):
    whole_ref, part_refs, (far_ref, acc_ref, w_ref, x_ref, sems) = rest[0], rest[1:-5], rest[-5:]
    count = w_ref.shape[0]
    units = arrived_ref.shape[0]
    groups = count // 16
    w_copies = [
        pltpu.make_async_copy(
            w_hbm.at[pl.ds(16 * g, 16)], w_ref.at[pl.ds(16 * g, 16)], sems.at[g]
        )
        for g in range(groups)
    ]
    acc_copy = pltpu.make_async_copy(acc_hbm, acc_ref, sems.at[groups])
    for copy in w_copies:
        copy.start()
    acc_copy.start()
    far_ref[...] = jnp.zeros_like(far_ref)
    for g in range(groups):
        for h in range(2):
            at = h * count + 16 * g
            x_ref[16 * g : 16 * g + 16, h * units : (h + 1) * units, :] = jnp.swapaxes(
                arrived_ref[:, at : at + 16, :], 0, 1
            )
    for g in range(groups):
        w_copies[g].wait()
        for inner in range(16):
            block = 16 * g + inner
            row = row_ref[block]
            far_ref[row] += jnp.dot(w_ref[block], x_ref[block], preferred_element_type=jnp.float32)
    acc_copy.wait()
    parts = len(part_refs)
    for k in range(parts):
        share = part_refs[k].shape[0]
        here = pl.ds(lax.rem(own_ref[0] + k, parts) * share, share)
        stepped = (time_step * (acc_ref[here] + far_ref[here])).astype(jnp.bfloat16)
        part_refs[k][...] = stepped
        whole_ref[here] = stepped


def far_product(own, remote_row, remote_w, acc, arrived, parts):
    count, side, _ = remote_w.shape
    block_rows, _, width = acc.shape
    vmem = pl.BlockSpec(memory_space=pltpu.VMEM)
    smem = pl.BlockSpec(memory_space=pltpu.SMEM)
    hbm = pl.BlockSpec(memory_space=pltpu.HBM)
    return pl.pallas_call(
        far_kernel,
        in_specs=[smem, smem, hbm, hbm, vmem],
        out_specs=[vmem] * (1 + parts),
        out_shape=[jax.ShapeDtypeStruct((block_rows, side, width), jnp.bfloat16)]
        + [jax.ShapeDtypeStruct((block_rows // parts, side, width), jnp.bfloat16)] * parts,
        scratch_shapes=[
            pltpu.VMEM((block_rows, side, width), jnp.float32),
            pltpu.VMEM((block_rows, side, width), jnp.float32),
            pltpu.VMEM((count, side, side), jnp.bfloat16),
            pltpu.VMEM((count, side, width), jnp.bfloat16),
            pltpu.SemaphoreType.DMA((count // 16 + 1,)),
        ],
        compiler_params=pltpu.CompilerParams(vmem_limit_bytes=24 * MIB),
        cost_estimate=pl.CostEstimate(
            flops=2 * count * side * side * width, bytes_accessed=8 * MIB, transcendentals=0
        ),
        name="far_blocks",
    )(own, remote_row, *in_hbm(remote_w, acc), arrived)


def cross(left, right):
    return lax.dot_general(
        left, right, (((0,), (0,)), ((), ())), preferred_element_type=jnp.float32
    )


def gram_kernel(own_ref, *refs):
    parts = len(refs) // 2
    x_refs, out_refs = refs[:parts], refs[parts:]
    side = x_refs[0].shape[1]
    half = side // 2
    for k in range(parts):
        device = lax.rem(own_ref[0] + k, parts)
        here, after, across = (x_refs[(-k - step) % parts][...] for step in (0, 1, 2))
        products = cross(here, jnp.concatenate([here, after, across], axis=1))
        out_refs[k][:side, :] = products[:, :side]
        out_refs[k][side : 2 * side, :] = products[:, side : 2 * side]
        last = products[:, 2 * side :]
        out_refs[k][2 * side :, :] = jnp.where(device < 2, last[:half], last.T[half:])


def gram_quarters(own, row_parts):
    parts = len(row_parts)
    rows, side = row_parts[0].shape
    vmem = pl.BlockSpec(memory_space=pltpu.VMEM)
    return pl.pallas_call(
        gram_kernel,
        in_specs=[pl.BlockSpec(memory_space=pltpu.SMEM)] + [vmem] * parts,
        out_specs=[vmem] * parts,
        out_shape=[jax.ShapeDtypeStruct((2 * side + side // 2, side), jnp.float32)] * parts,
        compiler_params=pltpu.CompilerParams(vmem_limit_bytes=16 * MIB),
        cost_estimate=pl.CostEstimate(
            flops=6 * parts * rows * side * side, bytes_accessed=2 * MIB, transcendentals=0
        ),
        name="gram_quarters",
    )(own, *row_parts)


def factor_block(matrix):
    side = matrix.shape[0]
    tiles = side // 8
    v = [matrix[8 * t : 8 * t + 8, :] for t in range(tiles)]
    lane = lax.broadcasted_iota(jnp.int32, (8, side), 1)
    sub = lax.broadcasted_iota(jnp.int32, (8, side), 0)
    inverse = []
    log_row = jnp.zeros((8, side), jnp.float32)
    for t0 in range(tiles):
        base = 8 * t0
        panel = v[t0]
        in_panel = (lane >= base) & (lane < base + 8)
        column = [jnp.broadcast_to(panel[:, base + q : base + q + 1], (8, side)) for q in range(8)]
        splat = [
            [jnp.broadcast_to(column[p][q : q + 1, :], (8, side)) for p in range(q + 1)]
            for q in range(8)
        ]
        recip, lower = [], [[None] * 8 for _ in range(8)]
        for p in range(8):
            recip.append(1.0 / splat[p][p])
            for q in range(p + 1, 8):
                lower[q][p] = splat[q][p] * recip[p]
            for q in range(p + 1, 8):
                for r in range(p + 1, q + 1):
                    splat[q][r] = splat[q][r] - lower[q][p] * splat[r][p]
        rows = []
        for q in range(8):
            own = jnp.broadcast_to(panel[q : q + 1, :], (8, side))
            own = jnp.where(in_panel, (lane == base + q).astype(jnp.float32), own)
            for p in range(q):
                own = own - lower[q][p] * rows[p]
            rows.append(own)
        for t in range(t0 + 1, tiles):
            reduced = []
            fresh = jnp.where(in_panel, 0.0, v[t])
            for p in range(8):
                mine = jnp.broadcast_to(v[t][:, base + p : base + p + 1], (8, side))
                for r in range(p):
                    mine = mine - lower[p][r] * reduced[r]
                reduced.append(mine)
                fresh = fresh - (mine * recip[p]) * rows[p]
            v[t] = fresh
        done, pivots = rows[0], splat[0][0]
        for q in range(1, 8):
            done = jnp.where(sub == q, rows[q], done)
            pivots = jnp.where(sub == q, splat[q][q], pivots)
        inverse.append(jnp.where(lane <= sub + base, done * lax.rsqrt(pivots), 0.0))
        log_row = log_row + jnp.where(lane == sub + base, 0.5 * jnp.log(pivots), 0.0)
    return jnp.concatenate(inverse, axis=0), jnp.sum(log_row, axis=0, keepdims=True)


def factor_kernel(scale, own_ref, *refs):
    inv_ref, log_ref, m_ref, z_ref = refs[-4:]
    parts = m_ref.shape[0]
    side = m_ref.shape[2]
    half = side // 2
    for a in range(parts):
        for b in range(a):
            m_ref[a, b] = jnp.zeros((side, side), jnp.float32)
    for k in range(parts):
        device = lax.rem(own_ref[0] + parts - k, parts)
        after = lax.rem(device + 1, parts)
        m_ref[device, device] = refs[k][:side, :] * scale
        second = refs[k][side : 2 * side, :] * scale
        m_ref[jnp.minimum(device, after), jnp.maximum(device, after)] = jnp.where(
            after < device, second.T, second
        )
        low = lax.rem(device, 2)
        m_ref[low, low + 2, pl.ds(pl.multiple_of(device // 2 * half, half), half), :] = (
            refs[k][2 * side :, :] * scale
        )
    sub = lax.broadcasted_iota(jnp.int32, (side, side), 0)
    lane = lax.broadcasted_iota(jnp.int32, (side, side), 1)
    eye = (sub == lane).astype(jnp.float32)

    @pl.loop(0, parts)
    def _(k):
        inverse, logs = factor_block(m_ref[k, k])
        log_ref[pl.ds(k, 1), :] = logs
        for b in range(parts):
            block = jnp.where(k == b, eye, m_ref[k, b])
            z_ref[b] = split_dot(inverse, block, 1, 0)
        for b in range(parts):
            inv_ref[k, b] = jnp.where(b <= k, z_ref[b], 0.0).astype(jnp.bfloat16)
        for a in range(1, parts):

            @pl.when(a > k)
            def _():
                for b in range(parts):
                    change = split_dot(z_ref[a], z_ref[b], 0, 0)
                    m_ref[a, b] = jnp.where(k == b, 0.0, m_ref[a, b]) - change


def cholesky_parts(own, quarters, unit_total):
    parts = len(quarters)
    side = quarters[0].shape[1]
    vmem = pl.BlockSpec(memory_space=pltpu.VMEM)
    return pl.pallas_call(
        functools.partial(factor_kernel, 1.0 / unit_total),
        in_specs=[pl.BlockSpec(memory_space=pltpu.SMEM)] + [vmem] * parts,
        out_specs=[vmem, vmem],
        out_shape=[
            jax.ShapeDtypeStruct((parts, parts, side, side), jnp.bfloat16),
            jax.ShapeDtypeStruct((parts, side), jnp.float32),
        ],
        scratch_shapes=[
            pltpu.VMEM((parts, parts, side, side), jnp.float32),
            pltpu.VMEM((parts, side, side), jnp.float32),
        ],
        compiler_params=pltpu.CompilerParams(vmem_limit_bytes=16 * MIB),
        cost_estimate=pl.CostEstimate(
            flops=200_000_000, bytes_accessed=2 * MIB, transcendentals=100_000
        ),
        name="factor",
    )(own, *quarters)


def renew_kernel(own_ref, *refs):
    x_refs, (inv_ref, out_hbm, out_ref, sems) = refs[:-4], refs[-4:]
    own = own_ref[0]
    parts = len(x_refs)
    chunks = sems.shape[0]
    chunk = out_ref.shape[0] // chunks
    inverse = jnp.concatenate(
        [inv_ref[own, lax.rem(own + parts - k, parts)] for k in range(parts)], axis=1
    )
    copies = []
    for c in range(chunks):
        here = pl.ds(c * chunk, chunk)
        vectors = jnp.concatenate([x_ref[here, :] for x_ref in x_refs], axis=1)
        out_ref[here, :] = lax.dot_general(
            vectors, inverse, (((1,), (1,)), ((), ())), preferred_element_type=jnp.float32
        ).astype(jnp.bfloat16)
        copies.append(pltpu.make_async_copy(out_ref.at[here], out_hbm.at[here], sems.at[c]))
        copies[c].start()
    for copy in copies:
        copy.wait()


def renew(own, vectors, inverse):
    parts = len(vectors)
    rows, width = vectors[0].shape
    side = inverse.shape[-1]
    vmem = pl.BlockSpec(memory_space=pltpu.VMEM)
    return pl.pallas_call(
        renew_kernel,
        in_specs=[pl.BlockSpec(memory_space=pltpu.SMEM)] + [vmem] * (parts + 1),
        out_specs=pl.BlockSpec(memory_space=pltpu.HBM),
        out_shape=pltpu.HBM((rows, side), jnp.bfloat16),
        scratch_shapes=[
            pltpu.VMEM((rows, side), jnp.bfloat16),
            pltpu.SemaphoreType.DMA((4,)),
        ],
        compiler_params=pltpu.CompilerParams(vmem_limit_bytes=16 * MIB),
        cost_estimate=pl.CostEstimate(
            flops=2 * parts * rows * width * side, bytes_accessed=6 * MIB, transcendentals=0
        ),
        name="renew",
    )(own, *vectors, inverse)


def around(parts, step):
    return [(i, (i + step) % parts) for i in range(parts)]


def body(
    tangents,
    state,
    gain,
    local_w,
    local_row,
    local_col,
    remote_w,
    remote_row,
    remote_owner,
    remote_offset,
):
    rows_dev, width = tangents.shape
    side = local_w.shape[1]
    block_rows = rows_dev // side
    units = lax.axis_size("unit")
    parts = lax.axis_size("vec")
    unit_total = float(rows_dev * units)

    assert side == 2 * units and units <= 256 and block_rows <= 256
    blocks = tangents.reshape(block_rows, side, width)
    far_count = remote_offset.shape[0]
    pieces, spread = spread_pieces(state, gain, blocks, remote_owner, remote_offset, units)
    table = lax.all_to_all(spread, "unit", 0, 0, tiled=True)
    asked = table[:, 2 * block_rows, :].astype(jnp.float32)
    index = asked[:, :far_count] * block_rows + asked[:, far_count:]
    chosen = pick_rows(index, table, block_rows)
    arrived = lax.all_to_all(chosen, "unit", 0, 0, tiled=True)

    own = lax.axis_index("vec").astype(jnp.int32).reshape(1)
    steps = (2, 1, 3)
    assert parts == 4
    acc = local_product(local_row, local_col, local_w, pieces, blocks)
    stepped, *outgoing = far_product(own, remote_row, remote_w, acc, arrived, parts)

    row_parts = [outgoing[0]] + [None] * 3
    for k in steps:
        row_parts[k] = lax.ppermute(outgoing[k], "vec", around(parts, k))
    row_parts = [part.reshape(rows_dev // parts, width) for part in row_parts]
    quarters = gram_quarters(own, row_parts)
    mine = quarters[0]
    for k in steps:
        mine = mine + lax.ppermute(quarters[k], "vec", around(parts, k))

    late, mine = lax.optimization_barrier((stepped.reshape(rows_dev, width), mine))
    vectors = [late] + [None] * 3
    for k in (1, 3):
        vectors[k] = lax.ppermute(late, "vec", around(parts, k))

    share = mine.size // units
    by_unit = lax.all_to_all(mine.reshape(units, 1, share), "unit", 0, 0, tiled=True)
    summed = jnp.sum(by_unit, axis=0, keepdims=True)
    spread_sum = jnp.broadcast_to(summed, (units, 1, share))
    quarter = lax.all_to_all(spread_sum, "unit", 0, 0, tiled=True).reshape(mine.shape)
    quarter, vectors[1], vectors[3] = lax.optimization_barrier((quarter, vectors[1], vectors[3]))
    gathered = [quarter] + [None] * 3
    for k in steps:
        gathered[k] = lax.ppermute(quarter, "vec", around(parts, k))

    later, gathered = lax.optimization_barrier((late, gathered))
    vectors[2] = lax.ppermute(later, "vec", around(parts, 2))
    inverse, logs = cholesky_parts(own, gathered, unit_total)
    renewed = renew(own, vectors, inverse)
    return (renewed, logs.reshape(parts * width))


def solution(mesh):
    placed = (
        P("unit", "vec"),
        P("unit"),
        P("unit"),
        P("unit", None, None),
        P("unit"),
        P("unit"),
        P("unit", None, None),
        P("unit"),
        P("unit", None),
        P("unit"),
    )
    return jax.shard_map(
        body, mesh=mesh, in_specs=placed, out_specs=(P("unit", "vec"), P()), check_vma=False
    )
```

```python
import functools

import jax
import jax.numpy as jnp
from jax import lax
from jax.experimental import pallas as pl
from jax.experimental.pallas import tpu as pltpu
from jax.sharding import PartitionSpec as P

time_step = 0.5
HIGHEST = lax.Precision.HIGHEST
MIB = 1024 * 1024


def split_dot(left, right, left_dim, right_dim):
    return lax.dot_general(
        left,
        right,
        (((left_dim,), (right_dim,)), ((), ())),
        precision=HIGHEST,
        preferred_element_type=jnp.float32,
    )


def local_kernel(row_ref, col_ref, w_ref, x_ref, t_ref, acc_ref):
    step = pl.program_id(0)
    count = w_ref.shape[0]

    @pl.when(step == 0)
    def _():
        acc_ref[...] = t_ref[...].astype(jnp.float32)

    @pl.loop(0, count // 8)
    def _(group):
        for inner in range(8):
            block = group * 8 + inner
            row = row_ref[step * count + block]
            col = col_ref[step * count + block]
            acc_ref[row] += jnp.dot(w_ref[block], x_ref[col], preferred_element_type=jnp.float32)


def local_product(local_row, local_col, local_w, pieces, tangents):
    count, side, _ = local_w.shape
    block_rows, _, width = pieces.shape
    chunk = 32
    whole = lambda i, *_: (0, 0, 0)
    return pl.pallas_call(
        local_kernel,
        grid_spec=pltpu.PrefetchScalarGridSpec(
            num_scalar_prefetch=2,
            grid=(count // chunk,),
            in_specs=[
                pl.BlockSpec((chunk, side, side), lambda i, *_: (i, 0, 0)),
                pl.BlockSpec((block_rows, side, width), whole),
                pl.BlockSpec((block_rows, side, width), whole),
            ],
            out_specs=pl.BlockSpec((block_rows, side, width), whole),
        ),
        out_shape=pltpu.HBM((block_rows, side, width), jnp.float32),
        compiler_params=pltpu.CompilerParams(vmem_limit_bytes=16 * MIB),
        cost_estimate=pl.CostEstimate(
            flops=2 * count * side * side * width, bytes_accessed=14 * MIB, transcendentals=0
        ),
        name="local_blocks",
    )(local_row, local_col, local_w, pieces, tangents)


def column_of(row, side):
    return jnp.broadcast_to(row, (side, side)).T


def spread_kernel(*refs):
    sources, (pieces_ref, spread_ref), targets, sems = refs[:5], refs[5:7], refs[7:12], refs[12]
    owner_ref, offset_ref, state_ref, gain_ref, t_ref = targets
    copies = [
        pltpu.make_async_copy(source, target, sems.at[i])
        for i, (source, target) in enumerate(zip(sources, targets))
    ]
    for copy in copies:
        copy.start()
    block_rows, side, width = t_ref.shape
    half = side // 2
    units, rows, _ = spread_ref.shape
    extra = rows - 2 * block_rows
    copies[0].wait()
    copies[1].wait()
    ask = jnp.concatenate([owner_ref[...], offset_ref[...]], axis=1).astype(jnp.float32)
    spread_ref[:, 2 * block_rows :, :] = jnp.broadcast_to(
        ask.reshape(1, 1, width), (units, extra, width)
    ).astype(jnp.bfloat16)
    copies[2].wait()
    copies[3].wait()
    gain = gain_ref[...]
    slopes = gain * (1.0 - jnp.tanh(gain * state_ref[...]) ** 2)
    copies[4].wait()
    for p in range(block_rows):
        slope = column_of(slopes[p : p + 1, :], side)
        pieces_ref[p] = (slope * t_ref[p].astype(jnp.float32)).astype(jnp.bfloat16)
    for h in range(2):
        for g in range(block_rows // 16):
            group = pieces_ref[16 * g : 16 * g + 16, h * half : (h + 1) * half, :]
            at = h * block_rows + 16 * g
            spread_ref[:, at : at + 16, :] = jnp.swapaxes(group, 0, 1)


def in_hbm(*arrays):
    return [pltpu.with_memory_space_constraint(array, pltpu.HBM) for array in arrays]


def spread_pieces(state, gain, blocks, owner, offset, units):
    block_rows, side, width = blocks.shape
    rows = 2 * block_rows + 8
    count = offset.shape[0]
    vmem = pl.BlockSpec(memory_space=pltpu.VMEM)
    hbm = pl.BlockSpec(memory_space=pltpu.HBM)
    return pl.pallas_call(
        spread_kernel,
        in_specs=[hbm] * 5,
        out_specs=[vmem] * 2,
        out_shape=[
            jax.ShapeDtypeStruct((block_rows, side, width), jnp.bfloat16),
            jax.ShapeDtypeStruct((units, rows, width), jnp.bfloat16),
        ],
        scratch_shapes=[
            pltpu.VMEM((1, count), jnp.int32),
            pltpu.VMEM((1, count), jnp.int32),
            pltpu.VMEM((block_rows, side), jnp.float32),
            pltpu.VMEM((block_rows, side), jnp.float32),
            pltpu.VMEM((block_rows, side, width), jnp.bfloat16),
            pltpu.SemaphoreType.DMA((5,)),
        ],
        compiler_params=pltpu.CompilerParams(vmem_limit_bytes=16 * MIB),
        cost_estimate=pl.CostEstimate(
            flops=4 * MIB, bytes_accessed=4 * MIB, transcendentals=block_rows * side
        ),
        name="spread_pieces",
    )(
        *in_hbm(
            owner.reshape(1, count),
            offset.reshape(1, count),
            state.reshape(block_rows, side),
            gain.reshape(block_rows, side),
            blocks,
        )
    )


def pick_kernel(block_rows, index_ref, table_ref, out_ref):
    shards, rows, width = out_ref.shape
    owners = table_ref.shape[0]
    depth = owners * block_rows
    table = jnp.concatenate(
        [
            table_ref[:, h * block_rows : (h + 1) * block_rows, :].reshape(depth, width)
            for h in range(2)
        ],
        axis=1,
    )
    index = jnp.concatenate(
        [column_of(index_ref[0, g : g + 1, :], width) for g in range(index_ref.shape[1])], axis=0
    ).astype(jnp.int32)
    lane = lax.broadcasted_iota(jnp.int32, index.shape, 1)
    hot = jnp.concatenate(
        [(index == lane + width * k).astype(jnp.bfloat16) for k in range(depth // width)], axis=1
    )
    found = jnp.dot(hot, table, preferred_element_type=jnp.float32).astype(jnp.bfloat16)
    found = found.reshape(shards, rows // 2, 2 * width)
    out_ref[:, : rows // 2, :] = found[:, :, :width]
    out_ref[:, rows // 2 :, :] = found[:, :, width:]


def pick_rows(index, table, block_rows):
    units, far_count = index.shape
    width = table.shape[-1]
    steps = 4
    lines = units * far_count // width // steps
    return pl.pallas_call(
        functools.partial(pick_kernel, block_rows),
        grid=(steps,),
        in_specs=[
            pl.BlockSpec((1, lines, width), lambda i: (i, 0, 0)),
            pl.BlockSpec(table.shape, lambda i: (0, 0, 0)),
        ],
        out_specs=pl.BlockSpec((units // steps, 2 * far_count, width), lambda i: (i, 0, 0)),
        out_shape=pltpu.HBM((units, 2 * far_count, width), jnp.bfloat16),
        compiler_params=pltpu.CompilerParams(vmem_limit_bytes=32 * MIB),
        cost_estimate=pl.CostEstimate(
            flops=4_000_000_000, bytes_accessed=4 * MIB, transcendentals=0
        ),
        name="pick_rows",
    )(index.reshape(steps, lines, width), table)


def far_kernel(own_ref, row_ref, w_hbm, acc_hbm, arrived_ref, *rest):
    whole_ref, half_refs, part_refs = rest[0], rest[1:3], rest[3:-5]
    far_ref, acc_ref, w_ref, x_ref, sems = rest[-5:]
    count = w_ref.shape[0]
    units = arrived_ref.shape[0]
    groups = count // 16
    w_copies = [
        pltpu.make_async_copy(
            w_hbm.at[pl.ds(16 * g, 16)], w_ref.at[pl.ds(16 * g, 16)], sems.at[g]
        )
        for g in range(groups)
    ]
    acc_copy = pltpu.make_async_copy(acc_hbm, acc_ref, sems.at[groups])
    for copy in w_copies:
        copy.start()
    acc_copy.start()
    far_ref[...] = jnp.zeros_like(far_ref)
    for g in range(groups):
        for h in range(2):
            at = h * count + 16 * g
            x_ref[16 * g : 16 * g + 16, h * units : (h + 1) * units, :] = jnp.swapaxes(
                arrived_ref[:, at : at + 16, :], 0, 1
            )
    for g in range(groups):
        w_copies[g].wait()
        for inner in range(16):
            block = 16 * g + inner
            row = row_ref[block]
            far_ref[row] += jnp.dot(w_ref[block], x_ref[block], preferred_element_type=jnp.float32)
    acc_copy.wait()
    whole_ref[...] = (time_step * (acc_ref[...] + far_ref[...])).astype(jnp.bfloat16)
    half_rows = half_refs[0].shape[0]
    for h in range(2):
        half_refs[h][...] = whole_ref[h * half_rows : (h + 1) * half_rows]
    parts = len(part_refs)
    for k in range(parts):
        share = part_refs[k].shape[0]
        part_refs[k][...] = whole_ref[pl.ds(lax.rem(own_ref[0] + k, parts) * share, share)]


def far_product(own, remote_row, remote_w, acc, arrived, parts):
    count, side, _ = remote_w.shape
    block_rows, _, width = acc.shape
    vmem = pl.BlockSpec(memory_space=pltpu.VMEM)
    smem = pl.BlockSpec(memory_space=pltpu.SMEM)
    hbm = pl.BlockSpec(memory_space=pltpu.HBM)
    return pl.pallas_call(
        far_kernel,
        in_specs=[smem, smem, hbm, hbm, vmem],
        out_specs=[vmem] * (3 + parts),
        out_shape=[jax.ShapeDtypeStruct((block_rows, side, width), jnp.bfloat16)]
        + [jax.ShapeDtypeStruct((block_rows // 2, side, width), jnp.bfloat16)] * 2
        + [jax.ShapeDtypeStruct((block_rows // parts, side, width), jnp.bfloat16)] * parts,
        scratch_shapes=[
            pltpu.VMEM((block_rows, side, width), jnp.float32),
            pltpu.VMEM((block_rows, side, width), jnp.float32),
            pltpu.VMEM((count, side, side), jnp.bfloat16),
            pltpu.VMEM((count, side, width), jnp.bfloat16),
            pltpu.SemaphoreType.DMA((count // 16 + 1,)),
        ],
        compiler_params=pltpu.CompilerParams(vmem_limit_bytes=24 * MIB),
        cost_estimate=pl.CostEstimate(
            flops=2 * count * side * side * width, bytes_accessed=8 * MIB, transcendentals=0
        ),
        name="far_blocks",
    )(own, remote_row, *in_hbm(remote_w, acc), arrived)


def cross(left, right):
    return lax.dot_general(
        left, right, (((0,), (0,)), ((), ())), preferred_element_type=jnp.float32
    )


def gram_kernel(own_ref, *refs):
    parts = len(refs) // 2
    x_refs, out_refs = refs[:parts], refs[parts:]
    side = x_refs[0].shape[1]
    half = side // 2
    for k in range(parts):
        device = lax.rem(own_ref[0] + k, parts)
        here, after, across = (x_refs[(-k - step) % parts][...] for step in (0, 1, 2))
        products = cross(here, jnp.concatenate([here, after, across], axis=1))
        out_refs[k][:side, :] = products[:, :side]
        out_refs[k][side : 2 * side, :] = products[:, side : 2 * side]
        last = products[:, 2 * side :]
        out_refs[k][2 * side :, :] = jnp.where(device < 2, last[:half], last.T[half:])


def gram_quarters(own, row_parts):
    parts = len(row_parts)
    rows, side = row_parts[0].shape
    vmem = pl.BlockSpec(memory_space=pltpu.VMEM)
    return pl.pallas_call(
        gram_kernel,
        in_specs=[pl.BlockSpec(memory_space=pltpu.SMEM)] + [vmem] * parts,
        out_specs=[vmem] * parts,
        out_shape=[jax.ShapeDtypeStruct((2 * side + side // 2, side), jnp.float32)] * parts,
        compiler_params=pltpu.CompilerParams(vmem_limit_bytes=16 * MIB),
        cost_estimate=pl.CostEstimate(
            flops=6 * parts * rows * side * side, bytes_accessed=2 * MIB, transcendentals=0
        ),
        name="gram_quarters",
    )(own, *row_parts)


def factor_block(matrix):
    side = matrix.shape[0]
    tiles = side // 8
    v = [matrix[8 * t : 8 * t + 8, :] for t in range(tiles)]
    lane = lax.broadcasted_iota(jnp.int32, (8, side), 1)
    sub = lax.broadcasted_iota(jnp.int32, (8, side), 0)
    inverse = []
    log_row = jnp.zeros((8, side), jnp.float32)
    for t0 in range(tiles):
        base = 8 * t0
        panel = v[t0]
        in_panel = (lane >= base) & (lane < base + 8)
        column = [jnp.broadcast_to(panel[:, base + q : base + q + 1], (8, side)) for q in range(8)]
        splat = [
            [jnp.broadcast_to(column[p][q : q + 1, :], (8, side)) for p in range(q + 1)]
            for q in range(8)
        ]
        recip, lower = [], [[None] * 8 for _ in range(8)]
        for p in range(8):
            recip.append(1.0 / splat[p][p])
            for q in range(p + 1, 8):
                lower[q][p] = splat[q][p] * recip[p]
            for q in range(p + 1, 8):
                for r in range(p + 1, q + 1):
                    splat[q][r] = splat[q][r] - lower[q][p] * splat[r][p]
        rows = []
        for q in range(8):
            own = jnp.broadcast_to(panel[q : q + 1, :], (8, side))
            own = jnp.where(in_panel, (lane == base + q).astype(jnp.float32), own)
            for p in range(q):
                own = own - lower[q][p] * rows[p]
            rows.append(own)
        done, pivots = rows[0], splat[0][0]
        for q in range(1, 8):
            done = jnp.where(sub == q, rows[q], done)
            pivots = jnp.where(sub == q, splat[q][q], pivots)
        done = done * lax.rsqrt(pivots)
        for t in range(t0 + 1, min(t0 + 3, tiles)):
            reduced = []
            fresh = jnp.where(in_panel, 0.0, v[t])
            for p in range(8):
                mine = jnp.broadcast_to(v[t][:, base + p : base + p + 1], (8, side))
                for r in range(p):
                    mine = mine - lower[p][r] * reduced[r]
                reduced.append(mine)
                fresh = fresh - (mine * recip[p]) * rows[p]
            v[t] = fresh
        if t0 + 3 < tiles:
            change = split_dot(done, done, 0, 0)
            for t in range(t0 + 3, tiles):
                v[t] = jnp.where(in_panel, 0.0, v[t]) - change[8 * t : 8 * t + 8, :]
        inverse.append(jnp.where(lane <= sub + base, done, 0.0))
        log_row = log_row + jnp.where(lane == sub + base, 0.5 * jnp.log(pivots), 0.0)
    return jnp.concatenate(inverse, axis=0), jnp.sum(log_row, axis=0, keepdims=True)


def factor_kernel(scale, own_ref, *refs):
    inv_ref, log_ref, m_ref, z_ref = refs[-4:]
    parts = m_ref.shape[0]
    side = m_ref.shape[2]
    half = side // 2
    for a in range(parts):
        for b in range(a):
            m_ref[a, b] = jnp.zeros((side, side), jnp.float32)
    for k in range(parts):
        device = lax.rem(own_ref[0] + parts - k, parts)
        after = lax.rem(device + 1, parts)
        m_ref[device, device] = refs[k][:side, :] * scale
        second = refs[k][side : 2 * side, :] * scale
        m_ref[jnp.minimum(device, after), jnp.maximum(device, after)] = jnp.where(
            after < device, second.T, second
        )
        low = lax.rem(device, 2)
        m_ref[low, low + 2, pl.ds(pl.multiple_of(device // 2 * half, half), half), :] = (
            refs[k][2 * side :, :] * scale
        )
    for k in range(parts):
        inverse, logs = factor_block(m_ref[k, k])
        log_ref[k : k + 1, :] = logs
        for b in range(parts):
            z_ref[b] = inverse if b == k else split_dot(inverse, m_ref[k, b], 1, 0)
        for b in range(parts):
            inv_ref[k, b] = (z_ref[b] if b <= k else jnp.zeros((side, side))).astype(jnp.bfloat16)
        for a in range(k + 1, parts):
            for b in range(parts):
                if b <= k or b >= a:
                    change = split_dot(z_ref[a], z_ref[b], 0, 0)
                    m_ref[a, b] = -change if b == k else m_ref[a, b] - change


def cholesky_parts(own, quarters, unit_total):
    parts = len(quarters)
    side = quarters[0].shape[1]
    vmem = pl.BlockSpec(memory_space=pltpu.VMEM)
    return pl.pallas_call(
        functools.partial(factor_kernel, 1.0 / unit_total),
        in_specs=[pl.BlockSpec(memory_space=pltpu.SMEM)] + [vmem] * parts,
        out_specs=[vmem, vmem],
        out_shape=[
            jax.ShapeDtypeStruct((parts, parts, side, side), jnp.bfloat16),
            jax.ShapeDtypeStruct((parts, side), jnp.float32),
        ],
        scratch_shapes=[
            pltpu.VMEM((parts, parts, side, side), jnp.float32),
            pltpu.VMEM((parts, side, side), jnp.float32),
        ],
        compiler_params=pltpu.CompilerParams(vmem_limit_bytes=16 * MIB),
        cost_estimate=pl.CostEstimate(
            flops=200_000_000, bytes_accessed=2 * MIB, transcendentals=100_000
        ),
        name="factor",
    )(own, *quarters)


def renew_kernel(own_ref, own_rows, back1, near2, far2, back3, inv_ref, out_hbm, out_ref, sems):
    own = own_ref[0]
    parts = inv_ref.shape[0]
    chunks = sems.shape[0]
    chunk = out_ref.shape[0] // chunks
    inverse = jnp.concatenate(
        [inv_ref[own, lax.rem(own + parts - k, parts)] for k in range(parts)], axis=1
    )
    copies = []
    for c in range(chunks):
        here = pl.ds(c * chunk, chunk)
        back2 = (near2, far2)[c // (chunks // 2)]
        rows2 = back2[pl.ds(c % (chunks // 2) * chunk, chunk), :]
        vectors = jnp.concatenate([own_rows[here, :], back1[here, :], rows2, back3[here, :]], axis=1)
        out_ref[here, :] = lax.dot_general(
            vectors, inverse, (((1,), (1,)), ((), ())), preferred_element_type=jnp.float32
        ).astype(jnp.bfloat16)
        copies.append(pltpu.make_async_copy(out_ref.at[here], out_hbm.at[here], sems.at[c]))
        copies[c].start()
    for copy in copies:
        copy.wait()


def renew(own, vectors, inverse):
    rows, width = vectors[0].shape
    parts, _, side, _ = inverse.shape
    vmem = pl.BlockSpec(memory_space=pltpu.VMEM)
    return pl.pallas_call(
        renew_kernel,
        in_specs=[pl.BlockSpec(memory_space=pltpu.SMEM)] + [vmem] * (len(vectors) + 1),
        out_specs=pl.BlockSpec(memory_space=pltpu.HBM),
        out_shape=pltpu.HBM((rows, side), jnp.bfloat16),
        scratch_shapes=[
            pltpu.VMEM((rows, side), jnp.bfloat16),
            pltpu.SemaphoreType.DMA((4,)),
        ],
        compiler_params=pltpu.CompilerParams(vmem_limit_bytes=16 * MIB),
        cost_estimate=pl.CostEstimate(
            flops=2 * parts * rows * width * side, bytes_accessed=6 * MIB, transcendentals=0
        ),
        name="renew",
    )(own, *vectors, inverse)


def around(parts, step):
    return [(i, (i + step) % parts) for i in range(parts)]


def body(
    tangents,
    state,
    gain,
    local_w,
    local_row,
    local_col,
    remote_w,
    remote_row,
    remote_owner,
    remote_offset,
):
    rows_dev, width = tangents.shape
    side = local_w.shape[1]
    block_rows = rows_dev // side
    units = lax.axis_size("unit")
    parts = lax.axis_size("vec")
    unit_total = float(rows_dev * units)

    assert side == 2 * units and units <= 256 and block_rows <= 256
    blocks = tangents.reshape(block_rows, side, width)
    far_count = remote_offset.shape[0]
    pieces, spread = spread_pieces(state, gain, blocks, remote_owner, remote_offset, units)
    table = lax.all_to_all(spread, "unit", 0, 0, tiled=True)
    asked = table[:, 2 * block_rows, :].astype(jnp.float32)
    index = asked[:, :far_count] * block_rows + asked[:, far_count:]
    chosen = pick_rows(index, table, block_rows)
    arrived = lax.all_to_all(chosen, "unit", 0, 0, tiled=True)

    own = lax.axis_index("vec").astype(jnp.int32).reshape(1)
    steps = (2, 1, 3)
    assert parts == 4
    acc = local_product(local_row, local_col, local_w, pieces, blocks)
    stepped, near, far, *outgoing = far_product(own, remote_row, remote_w, acc, arrived, parts)

    row_parts = [outgoing[0]] + [None] * 3
    for k in steps:
        row_parts[k] = lax.ppermute(outgoing[k], "vec", around(parts, k))
    row_parts = [part.reshape(rows_dev // parts, width) for part in row_parts]
    quarters = gram_quarters(own, row_parts)
    mine = quarters[0]
    for k in steps:
        mine = mine + lax.ppermute(quarters[k], "vec", around(parts, k))

    stepped, mine = lax.optimization_barrier((stepped, mine))
    back1, back3 = (lax.ppermute(stepped, "vec", around(parts, k)) for k in (1, 3))

    share = mine.size // units
    by_unit = lax.all_to_all(mine.reshape(units, 1, share), "unit", 0, 0, tiled=True)
    summed = jnp.sum(by_unit, axis=0, keepdims=True)
    near, summed = lax.optimization_barrier((near, summed))
    near2 = lax.ppermute(near, "vec", around(parts, 2))
    spread_sum = jnp.broadcast_to(summed, (units, 1, share))
    quarter = lax.all_to_all(spread_sum, "unit", 0, 0, tiled=True).reshape(mine.shape)
    quarter, back1, back3, near2 = lax.optimization_barrier((quarter, back1, back3, near2))
    gathered = [quarter] + [None] * 3
    for k in steps:
        gathered[k] = lax.ppermute(quarter, "vec", around(parts, k))

    far, gathered = lax.optimization_barrier((far, gathered))
    far2 = lax.ppermute(far, "vec", around(parts, 2))
    inverse, logs = cholesky_parts(own, gathered, unit_total)
    vectors = [rows.reshape(-1, width) for rows in (stepped, back1, near2, far2, back3)]
    renewed = renew(own, vectors, inverse)
    return (renewed, logs.reshape(parts * width))


def solution(mesh):
    placed = (
        P("unit", "vec"),
        P("unit"),
        P("unit"),
        P("unit", None, None),
        P("unit"),
        P("unit"),
        P("unit", None, None),
        P("unit"),
        P("unit", None),
        P("unit"),
    )
    return jax.shard_map(
        body, mesh=mesh, in_specs=placed, out_specs=(P("unit", "vec"), P()), check_vma=False
    )
```

```python
import functools

import jax
import jax.numpy as jnp
from jax import lax
from jax.experimental import pallas as pl
from jax.experimental.pallas import tpu as pltpu
from jax.sharding import PartitionSpec as P

time_step = 0.5
HIGHEST = lax.Precision.HIGHEST
MIB = 1024 * 1024


def split_dot(left, right, left_dim, right_dim):
    return lax.dot_general(
        left,
        right,
        (((left_dim,), (right_dim,)), ((), ())),
        precision=HIGHEST,
        preferred_element_type=jnp.float32,
    )


def local_kernel(row_ref, col_ref, w_ref, x_ref, t_ref, acc_ref):
    step = pl.program_id(0)
    count = w_ref.shape[0]

    @pl.when(step == 0)
    def _():
        acc_ref[...] = t_ref[...].astype(jnp.float32)

    @pl.loop(0, count // 8)
    def _(group):
        for inner in range(8):
            block = group * 8 + inner
            row = row_ref[step * count + block]
            col = col_ref[step * count + block]
            acc_ref[row] += jnp.dot(w_ref[block], x_ref[col], preferred_element_type=jnp.float32)


def local_product(local_row, local_col, local_w, pieces, tangents):
    count, side, _ = local_w.shape
    block_rows, _, width = pieces.shape
    chunk = 32
    whole = lambda i, *_: (0, 0, 0)
    return pl.pallas_call(
        local_kernel,
        grid_spec=pltpu.PrefetchScalarGridSpec(
            num_scalar_prefetch=2,
            grid=(count // chunk,),
            in_specs=[
                pl.BlockSpec((chunk, side, side), lambda i, *_: (i, 0, 0)),
                pl.BlockSpec((block_rows, side, width), whole),
                pl.BlockSpec((block_rows, side, width), whole),
            ],
            out_specs=pl.BlockSpec((block_rows, side, width), whole),
        ),
        out_shape=pltpu.HBM((block_rows, side, width), jnp.float32),
        compiler_params=pltpu.CompilerParams(vmem_limit_bytes=16 * MIB),
        cost_estimate=pl.CostEstimate(
            flops=2 * count * side * side * width, bytes_accessed=14 * MIB, transcendentals=0
        ),
        name="local_blocks",
    )(local_row, local_col, local_w, pieces, tangents)


def column_of(row, side):
    return jnp.broadcast_to(row, (side, side)).T


def spread_kernel(*refs):
    sources, (pieces_ref, spread_ref), targets, sems = refs[:5], refs[5:7], refs[7:12], refs[12]
    owner_ref, offset_ref, state_ref, gain_ref, t_ref = targets
    copies = [
        pltpu.make_async_copy(source, target, sems.at[i])
        for i, (source, target) in enumerate(zip(sources, targets))
    ]
    for copy in copies:
        copy.start()
    block_rows, side, width = t_ref.shape
    half = side // 2
    units, rows, _ = spread_ref.shape
    extra = rows - 2 * block_rows
    copies[0].wait()
    copies[1].wait()
    ask = jnp.concatenate([owner_ref[...], offset_ref[...]], axis=1).astype(jnp.float32)
    spread_ref[:, 2 * block_rows :, :] = jnp.broadcast_to(
        ask.reshape(1, 1, width), (units, extra, width)
    ).astype(jnp.bfloat16)
    copies[2].wait()
    copies[3].wait()
    gain = gain_ref[...]
    slopes = gain * (1.0 - jnp.tanh(gain * state_ref[...]) ** 2)
    copies[4].wait()
    for p in range(block_rows):
        slope = column_of(slopes[p : p + 1, :], side)
        pieces_ref[p] = (slope * t_ref[p].astype(jnp.float32)).astype(jnp.bfloat16)
    for h in range(2):
        for g in range(block_rows // 16):
            group = pieces_ref[16 * g : 16 * g + 16, h * half : (h + 1) * half, :]
            at = h * block_rows + 16 * g
            spread_ref[:, at : at + 16, :] = jnp.swapaxes(group, 0, 1)


def in_hbm(*arrays):
    return [pltpu.with_memory_space_constraint(array, pltpu.HBM) for array in arrays]


def spread_pieces(state, gain, blocks, owner, offset, units):
    block_rows, side, width = blocks.shape
    rows = 2 * block_rows + 8
    count = offset.shape[0]
    vmem = pl.BlockSpec(memory_space=pltpu.VMEM)
    hbm = pl.BlockSpec(memory_space=pltpu.HBM)
    return pl.pallas_call(
        spread_kernel,
        in_specs=[hbm] * 5,
        out_specs=[vmem] * 2,
        out_shape=[
            jax.ShapeDtypeStruct((block_rows, side, width), jnp.bfloat16),
            jax.ShapeDtypeStruct((units, rows, width), jnp.bfloat16),
        ],
        scratch_shapes=[
            pltpu.VMEM((1, count), jnp.int32),
            pltpu.VMEM((1, count), jnp.int32),
            pltpu.VMEM((block_rows, side), jnp.float32),
            pltpu.VMEM((block_rows, side), jnp.float32),
            pltpu.VMEM((block_rows, side, width), jnp.bfloat16),
            pltpu.SemaphoreType.DMA((5,)),
        ],
        compiler_params=pltpu.CompilerParams(vmem_limit_bytes=16 * MIB),
        cost_estimate=pl.CostEstimate(
            flops=4 * MIB, bytes_accessed=4 * MIB, transcendentals=block_rows * side
        ),
        name="spread_pieces",
    )(
        *in_hbm(
            owner.reshape(1, count),
            offset.reshape(1, count),
            state.reshape(block_rows, side),
            gain.reshape(block_rows, side),
            blocks,
        )
    )


def pick_kernel(block_rows, index_ref, table_ref, out_ref):
    shards, rows, width = out_ref.shape
    owners = table_ref.shape[0]
    depth = owners * block_rows
    table = jnp.concatenate(
        [
            table_ref[:, h * block_rows : (h + 1) * block_rows, :].reshape(depth, width)
            for h in range(2)
        ],
        axis=1,
    )
    index = jnp.concatenate(
        [column_of(index_ref[0, g : g + 1, :], width) for g in range(index_ref.shape[1])], axis=0
    ).astype(jnp.int32)
    lane = lax.broadcasted_iota(jnp.int32, index.shape, 1)
    hot = jnp.concatenate(
        [(index == lane + width * k).astype(jnp.bfloat16) for k in range(depth // width)], axis=1
    )
    found = jnp.dot(hot, table, preferred_element_type=jnp.float32).astype(jnp.bfloat16)
    found = found.reshape(shards, rows // 2, 2 * width)
    out_ref[:, : rows // 2, :] = found[:, :, :width]
    out_ref[:, rows // 2 :, :] = found[:, :, width:]


def pick_rows(index, table, block_rows):
    units, far_count = index.shape
    width = table.shape[-1]
    steps = 2
    lines = units * far_count // width // steps
    return pl.pallas_call(
        functools.partial(pick_kernel, block_rows),
        grid=(steps,),
        in_specs=[
            pl.BlockSpec((1, lines, width), lambda i: (i, 0, 0)),
            pl.BlockSpec(table.shape, lambda i: (0, 0, 0)),
        ],
        out_specs=pl.BlockSpec((units // steps, 2 * far_count, width), lambda i: (i, 0, 0)),
        out_shape=pltpu.HBM((units, 2 * far_count, width), jnp.bfloat16),
        compiler_params=pltpu.CompilerParams(vmem_limit_bytes=32 * MIB),
        cost_estimate=pl.CostEstimate(
            flops=4_000_000_000, bytes_accessed=4 * MIB, transcendentals=0
        ),
        name="pick_rows",
    )(index.reshape(steps, lines, width), table)


def far_kernel(own_ref, row_ref, w_hbm, acc_hbm, arrived_ref, *rest):
    whole_ref, half_refs, part_refs = rest[0], rest[1:3], rest[3:-5]
    far_ref, acc_ref, w_ref, x_ref, sems = rest[-5:]
    count = w_ref.shape[0]
    units = arrived_ref.shape[0]
    groups = count // 16
    w_copies = [
        pltpu.make_async_copy(
            w_hbm.at[pl.ds(16 * g, 16)], w_ref.at[pl.ds(16 * g, 16)], sems.at[g]
        )
        for g in range(groups)
    ]
    acc_copy = pltpu.make_async_copy(acc_hbm, acc_ref, sems.at[groups])
    for copy in w_copies:
        copy.start()
    acc_copy.start()
    far_ref[...] = jnp.zeros_like(far_ref)
    for g in range(groups):
        for h in range(2):
            at = h * count + 16 * g
            x_ref[16 * g : 16 * g + 16, h * units : (h + 1) * units, :] = jnp.swapaxes(
                arrived_ref[:, at : at + 16, :], 0, 1
            )
    for g in range(groups):
        w_copies[g].wait()
        for inner in range(16):
            block = 16 * g + inner
            row = row_ref[block]
            far_ref[row] += jnp.dot(w_ref[block], x_ref[block], preferred_element_type=jnp.float32)
    acc_copy.wait()
    whole_ref[...] = (time_step * (acc_ref[...] + far_ref[...])).astype(jnp.bfloat16)
    half_rows = half_refs[0].shape[0]
    for h in range(2):
        half_refs[h][...] = whole_ref[h * half_rows : (h + 1) * half_rows]
    parts = len(part_refs)
    for k in range(parts):
        share = part_refs[k].shape[0]
        part_refs[k][...] = whole_ref[pl.ds(lax.rem(own_ref[0] + k, parts) * share, share)]


def far_product(own, remote_row, remote_w, acc, arrived, parts):
    count, side, _ = remote_w.shape
    block_rows, _, width = acc.shape
    vmem = pl.BlockSpec(memory_space=pltpu.VMEM)
    smem = pl.BlockSpec(memory_space=pltpu.SMEM)
    hbm = pl.BlockSpec(memory_space=pltpu.HBM)
    return pl.pallas_call(
        far_kernel,
        in_specs=[smem, smem, hbm, hbm, vmem],
        out_specs=[vmem] * (3 + parts),
        out_shape=[jax.ShapeDtypeStruct((block_rows, side, width), jnp.bfloat16)]
        + [jax.ShapeDtypeStruct((block_rows // 2, side, width), jnp.bfloat16)] * 2
        + [jax.ShapeDtypeStruct((block_rows // parts, side, width), jnp.bfloat16)] * parts,
        scratch_shapes=[
            pltpu.VMEM((block_rows, side, width), jnp.float32),
            pltpu.VMEM((block_rows, side, width), jnp.float32),
            pltpu.VMEM((count, side, side), jnp.bfloat16),
            pltpu.VMEM((count, side, width), jnp.bfloat16),
            pltpu.SemaphoreType.DMA((count // 16 + 1,)),
        ],
        compiler_params=pltpu.CompilerParams(vmem_limit_bytes=24 * MIB),
        cost_estimate=pl.CostEstimate(
            flops=2 * count * side * side * width, bytes_accessed=8 * MIB, transcendentals=0
        ),
        name="far_blocks",
    )(own, remote_row, *in_hbm(remote_w, acc), arrived)


def cross(left, right):
    return lax.dot_general(
        left, right, (((0,), (0,)), ((), ())), preferred_element_type=jnp.float32
    )


def gram_kernel(own_ref, *refs):
    parts = len(refs) // 2
    x_refs, out_refs = refs[:parts], refs[parts:]
    side = x_refs[0].shape[1]
    half = side // 2
    for k in range(parts):
        device = lax.rem(own_ref[0] + k, parts)
        here, after, across = (x_refs[(-k - step) % parts][...] for step in (0, 1, 2))
        products = cross(here, jnp.concatenate([here, after, across], axis=1))
        out_refs[k][:side, :] = products[:, :side]
        out_refs[k][side : 2 * side, :] = products[:, side : 2 * side]
        last = products[:, 2 * side :]
        out_refs[k][2 * side :, :] = jnp.where(device < 2, last[:half], last.T[half:])


def gram_quarters(own, row_parts):
    parts = len(row_parts)
    rows, side = row_parts[0].shape
    vmem = pl.BlockSpec(memory_space=pltpu.VMEM)
    return pl.pallas_call(
        gram_kernel,
        in_specs=[pl.BlockSpec(memory_space=pltpu.SMEM)] + [vmem] * parts,
        out_specs=[vmem] * parts,
        out_shape=[jax.ShapeDtypeStruct((2 * side + side // 2, side), jnp.float32)] * parts,
        compiler_params=pltpu.CompilerParams(vmem_limit_bytes=16 * MIB),
        cost_estimate=pl.CostEstimate(
            flops=6 * parts * rows * side * side, bytes_accessed=2 * MIB, transcendentals=0
        ),
        name="gram_quarters",
    )(own, *row_parts)


def factor_block(matrix):
    side = matrix.shape[0]
    tiles = side // 8
    v = [matrix[8 * t : 8 * t + 8, :] for t in range(tiles)]
    lane = lax.broadcasted_iota(jnp.int32, (8, side), 1)
    sub = lax.broadcasted_iota(jnp.int32, (8, side), 0)
    inverse = []
    log_row = jnp.zeros((8, side), jnp.float32)
    for t0 in range(tiles):
        base = 8 * t0
        panel = v[t0]
        in_panel = (lane >= base) & (lane < base + 8)
        column = [jnp.broadcast_to(panel[:, base + q : base + q + 1], (8, side)) for q in range(8)]
        splat = [
            [jnp.broadcast_to(column[p][q : q + 1, :], (8, side)) for p in range(q + 1)]
            for q in range(8)
        ]
        recip, lower = [], [[None] * 8 for _ in range(8)]
        for p in range(8):
            recip.append(1.0 / splat[p][p])
            for q in range(p + 1, 8):
                lower[q][p] = splat[q][p] * recip[p]
            for q in range(p + 1, 8):
                for r in range(p + 1, q + 1):
                    splat[q][r] = splat[q][r] - lower[q][p] * splat[r][p]
        rows = []
        for q in range(8):
            own = jnp.broadcast_to(panel[q : q + 1, :], (8, side))
            own = jnp.where(in_panel, (lane == base + q).astype(jnp.float32), own)
            for p in range(q):
                own = own - lower[q][p] * rows[p]
            rows.append(own)
        done, pivots = rows[0], splat[0][0]
        for q in range(1, 8):
            done = jnp.where(sub == q, rows[q], done)
            pivots = jnp.where(sub == q, splat[q][q], pivots)
        done = done * lax.rsqrt(pivots)
        for t in range(t0 + 1, min(t0 + 3, tiles)):
            reduced = []
            fresh = jnp.where(in_panel, 0.0, v[t])
            for p in range(8):
                mine = jnp.broadcast_to(v[t][:, base + p : base + p + 1], (8, side))
                for r in range(p):
                    mine = mine - lower[p][r] * reduced[r]
                reduced.append(mine)
                fresh = fresh - (mine * recip[p]) * rows[p]
            v[t] = fresh
        if t0 + 3 < tiles:
            change = split_dot(done, done, 0, 0)
            for t in range(t0 + 3, tiles):
                v[t] = jnp.where(in_panel, 0.0, v[t]) - change[8 * t : 8 * t + 8, :]
        inverse.append(jnp.where(lane <= sub + base, done, 0.0))
        log_row = log_row + jnp.where(lane == sub + base, 0.5 * jnp.log(pivots), 0.0)
    return jnp.concatenate(inverse, axis=0), jnp.sum(log_row, axis=0, keepdims=True)


def factor_kernel(scale, own_ref, *refs):
    inv_ref, log_ref, m_ref, z_ref = refs[-4:]
    parts = m_ref.shape[0]
    side = m_ref.shape[2]
    half = side // 2
    for k in range(parts):
        device = lax.rem(own_ref[0] + parts - k, parts)
        after = lax.rem(device + 1, parts)
        m_ref[device, device] = refs[k][:side, :] * scale
        second = refs[k][side : 2 * side, :] * scale
        m_ref[jnp.minimum(device, after), jnp.maximum(device, after)] = jnp.where(
            after < device, second.T, second
        )
        low = lax.rem(device, 2)
        m_ref[low, low + 2, pl.ds(pl.multiple_of(device // 2 * half, half), half), :] = (
            refs[k][2 * side :, :] * scale
        )
    for k in range(parts):
        inverse, logs = factor_block(m_ref[k, k])
        log_ref[k : k + 1, :] = logs
        for b in range(parts):
            z_ref[b] = inverse if b == k else split_dot(inverse, m_ref[k, b], 1, 0)
        for b in range(parts):
            inv_ref[k, b] = (z_ref[b] if b <= k else jnp.zeros((side, side))).astype(jnp.bfloat16)
        for a in range(k + 1, parts):
            for b in range(parts):
                if b <= k or b >= a:
                    change = split_dot(z_ref[a], z_ref[b], 0, 0)
                    m_ref[a, b] = -change if b == k else m_ref[a, b] - change


def cholesky_parts(own, quarters, unit_total):
    parts = len(quarters)
    side = quarters[0].shape[1]
    vmem = pl.BlockSpec(memory_space=pltpu.VMEM)
    return pl.pallas_call(
        functools.partial(factor_kernel, 1.0 / unit_total),
        in_specs=[pl.BlockSpec(memory_space=pltpu.SMEM)] + [vmem] * parts,
        out_specs=[vmem, vmem],
        out_shape=[
            jax.ShapeDtypeStruct((parts, parts, side, side), jnp.bfloat16),
            jax.ShapeDtypeStruct((parts, side), jnp.float32),
        ],
        scratch_shapes=[
            pltpu.VMEM((parts, parts, side, side), jnp.float32),
            pltpu.VMEM((parts, side, side), jnp.float32),
        ],
        compiler_params=pltpu.CompilerParams(vmem_limit_bytes=16 * MIB),
        cost_estimate=pl.CostEstimate(
            flops=200_000_000, bytes_accessed=2 * MIB, transcendentals=100_000
        ),
        name="factor",
    )(own, *quarters)


def renew_kernel(own_ref, own_rows, back1, near2, far2, back3, inv_ref, out_hbm, out_ref, sems):
    own = own_ref[0]
    parts = inv_ref.shape[0]
    chunks = sems.shape[0]
    chunk = out_ref.shape[0] // chunks
    inverse = jnp.concatenate(
        [inv_ref[own, lax.rem(own + parts - k, parts)] for k in range(parts)], axis=1
    )
    copies = []
    for c in range(chunks):
        here = pl.ds(c * chunk, chunk)
        back2 = (near2, far2)[c // (chunks // 2)]
        rows2 = back2[pl.ds(c % (chunks // 2) * chunk, chunk), :]
        vectors = jnp.concatenate([own_rows[here, :], back1[here, :], rows2, back3[here, :]], axis=1)
        out_ref[here, :] = lax.dot_general(
            vectors, inverse, (((1,), (1,)), ((), ())), preferred_element_type=jnp.float32
        ).astype(jnp.bfloat16)
        copies.append(pltpu.make_async_copy(out_ref.at[here], out_hbm.at[here], sems.at[c]))
        copies[c].start()
    for copy in copies:
        copy.wait()


def renew(own, vectors, inverse):
    rows, width = vectors[0].shape
    parts, _, side, _ = inverse.shape
    vmem = pl.BlockSpec(memory_space=pltpu.VMEM)
    return pl.pallas_call(
        renew_kernel,
        in_specs=[pl.BlockSpec(memory_space=pltpu.SMEM)] + [vmem] * (len(vectors) + 1),
        out_specs=pl.BlockSpec(memory_space=pltpu.HBM),
        out_shape=pltpu.HBM((rows, side), jnp.bfloat16),
        scratch_shapes=[
            pltpu.VMEM((rows, side), jnp.bfloat16),
            pltpu.SemaphoreType.DMA((4,)),
        ],
        compiler_params=pltpu.CompilerParams(vmem_limit_bytes=16 * MIB),
        cost_estimate=pl.CostEstimate(
            flops=2 * parts * rows * width * side, bytes_accessed=6 * MIB, transcendentals=0
        ),
        name="renew",
    )(own, *vectors, inverse)


def around(parts, step):
    return [(i, (i + step) % parts) for i in range(parts)]


def body(
    tangents,
    state,
    gain,
    local_w,
    local_row,
    local_col,
    remote_w,
    remote_row,
    remote_owner,
    remote_offset,
):
    rows_dev, width = tangents.shape
    side = local_w.shape[1]
    block_rows = rows_dev // side
    units = lax.axis_size("unit")
    parts = lax.axis_size("vec")
    unit_total = float(rows_dev * units)

    assert side == 2 * units and units <= 256 and block_rows <= 256
    blocks = tangents.reshape(block_rows, side, width)
    far_count = remote_offset.shape[0]
    pieces, spread = spread_pieces(state, gain, blocks, remote_owner, remote_offset, units)
    table = lax.all_to_all(spread, "unit", 0, 0, tiled=True)
    asked = table[:, 2 * block_rows, :].astype(jnp.float32)
    index = asked[:, :far_count] * block_rows + asked[:, far_count:]
    chosen = pick_rows(index, table, block_rows)
    arrived = lax.all_to_all(chosen, "unit", 0, 0, tiled=True)

    own = lax.axis_index("vec").astype(jnp.int32).reshape(1)
    steps = (2, 1, 3)
    assert parts == 4
    acc = local_product(local_row, local_col, local_w, pieces, blocks)
    stepped, near, far, *outgoing = far_product(own, remote_row, remote_w, acc, arrived, parts)

    row_parts = [outgoing[0]] + [None] * 3
    for k in steps:
        row_parts[k] = lax.ppermute(outgoing[k], "vec", around(parts, k))
    row_parts = [part.reshape(rows_dev // parts, width) for part in row_parts]
    quarters = gram_quarters(own, row_parts)
    mine = quarters[0]
    for k in steps:
        mine = mine + lax.ppermute(quarters[k], "vec", around(parts, k))

    stepped, mine = lax.optimization_barrier((stepped, mine))
    back1, back3 = (lax.ppermute(stepped, "vec", around(parts, k)) for k in (1, 3))

    share = mine.size // units
    by_unit = lax.all_to_all(mine.reshape(units, 1, share), "unit", 0, 0, tiled=True)
    summed = jnp.sum(by_unit, axis=0, keepdims=True)
    near, summed = lax.optimization_barrier((near, summed))
    near2 = lax.ppermute(near, "vec", around(parts, 2))
    spread_sum = jnp.broadcast_to(summed, (units, 1, share))
    quarter = lax.all_to_all(spread_sum, "unit", 0, 0, tiled=True).reshape(mine.shape)
    quarter, back1, back3, near2 = lax.optimization_barrier((quarter, back1, back3, near2))
    gathered = [quarter] + [None] * 3
    for k in steps:
        gathered[k] = lax.ppermute(quarter, "vec", around(parts, k))

    far, gathered = lax.optimization_barrier((far, gathered))
    far2 = lax.ppermute(far, "vec", around(parts, 2))
    inverse, logs = cholesky_parts(own, gathered, unit_total)
    vectors = [rows.reshape(-1, width) for rows in (stepped, back1, near2, far2, back3)]
    renewed = renew(own, vectors, inverse)
    return (renewed, logs.reshape(parts * width))


def solution(mesh):
    placed = (
        P("unit", "vec"),
        P("unit"),
        P("unit"),
        P("unit", None, None),
        P("unit"),
        P("unit"),
        P("unit", None, None),
        P("unit"),
        P("unit", None),
        P("unit"),
    )
    return jax.shard_map(
        body, mesh=mesh, in_specs=placed, out_specs=(P("unit", "vec"), P()), check_vma=False
    )
```
